512 devices in a mesh: dp: 64 (over z, x), sub: 8 (over y, core).
Axes of the slice: x: 4, y: 4, z: 16, core: 2. Of those that a mesh axis runs over, the one named last changes fastest.
Arguments:
- points: bfloat16 [262144, 256], P(('dp', 'sub'))
- candidates: int32 [4, 768], replicated, may hold values from 0 to 262143, as said below
- owner_slot: int32 [3072], replicated, may hold values from 0 to 3071, each once
Outputs:
- centroids: float32 [3072, 256], P(('dp', 'sub'))
- masses: float32 [3072], P(('dp', 'sub'))
- min_dist: float32 [262144], P(('dp', 'sub'))
The draws below stay inside these ranges and needn't reach their ends.
Inputs may be any that keep to these rules, and one draw needn't show every extreme that they name: In each round the candidates are distinct rows; no device's block of 512 rows holds more than 8 candidates of one round, and in each round some device's block holds exactly 8.
All inputs are finite; a program needn't handle non-finite values.
Results may differ from the reference program's by a relative error of at most 0.00055.
Values may be sent and summed in bfloat16 or wider, within the bound.
A program may use at most 64 MiB of HBM per device.

```python
import jax
import jax.numpy as jnp
from jax import lax

DIM = 256
CAND = 768
ROUNDS = 4
ROWS_DEV = 512
NPTS = 262144
TOTAL = 3072
MOST = 8
CLUSTER = 128


def draw_points(key, part):
    key_center, key_noise = jax.random.split(key, 2)
    groups = NPTS // CLUSTER
    centers = jax.random.normal(key_center, (groups, DIM), jnp.float32) * DIM ** (-0.5)
    noise = jax.random.normal(key_noise, (NPTS, DIM), jnp.float32) * 0.5 * DIM ** (-0.5)
    values = jnp.repeat(centers, CLUSTER, axis=0) + noise
    return values.astype(jnp.bfloat16)


def draw_candidates(key, part):
    device_count = NPTS // ROWS_DEV
    span = ROWS_DEV // MOST
    rounds_out = []
    for which_round in range(ROUNDS):
        round_key = jax.random.fold_in(key, which_round + 17)
        key_perm, key_row, key_order = jax.random.split(round_key, 3)
        device_perm = jax.random.permutation(key_perm, device_count).astype(jnp.int32)
        positions = jnp.arange(CAND, dtype=jnp.int32)
        heavy = positions < MOST
        others = positions - MOST
        owner_pos = jnp.where(heavy, 0, 1 + others % (device_count - 1))
        slot_no = jnp.where(heavy, positions, others // (device_count - 1))
        owner_dev = device_perm[owner_pos]
        offset = jax.random.randint(key_row, (CAND,), 0, span, jnp.int32)
        row_index = owner_dev * ROWS_DEV + slot_no * span + offset
        order = jax.random.permutation(key_order, CAND)
        rounds_out.append(row_index[order].astype(jnp.int32))
    return jnp.stack(rounds_out, axis=0)


def setup_inputs(seed: int = 0) -> dict:
    arg_keys = jax.random.split(jax.random.key(seed), 4)
    points = draw_points(jax.random.fold_in(arg_keys[3], 71), 0)
    candidates = draw_candidates(jax.random.fold_in(arg_keys[3], 71), 0)
    owner_slot = jax.random.permutation(arg_keys[2], TOTAL).astype(jnp.int32)
    return dict(points=points, candidates=candidates, owner_slot=owner_slot)


def reference(points, candidates, owner_slot):
    chosen = points[candidates.reshape(-1)]
    cand_norm = jnp.sum(chosen.astype(jnp.float32) ** 2, axis=1)
    block_rows = min(4096, NPTS)
    blocks = points.reshape(NPTS // block_rows, block_rows, DIM)

    def one_block(carry, piece):
        sums_acc, mass_acc = carry
        point_norm = jnp.sum(piece.astype(jnp.float32) ** 2, axis=1)
        dots = lax.dot_general(piece, chosen, (((1,), (1,)), ((), ())), preferred_element_type=jnp.float32)
        dist = point_norm[:, None] + cand_norm[None, :] - 2.0 * dots
        nearest = jnp.min(dist, axis=1)
        kernel = jnp.exp(-dist / 0.25).astype(jnp.bfloat16)
        sums_acc = sums_acc + lax.dot_general(kernel, piece, (((0,), (0,)), ((), ())), preferred_element_type=jnp.float32)
        mass_acc = mass_acc + jnp.sum(kernel.astype(jnp.float32), axis=0)
        return (sums_acc, mass_acc), nearest

    start = (jnp.zeros((TOTAL, DIM), jnp.float32), jnp.zeros((TOTAL,), jnp.float32))
    (sums, mass), nearest = lax.scan(one_block, start, blocks)
    centroids = jnp.zeros((TOTAL, DIM), jnp.float32).at[owner_slot].set(sums / mass[:, None])
    masses = jnp.zeros((TOTAL,), jnp.float32).at[owner_slot].set(mass)
    return centroids, masses, nearest.reshape(NPTS)
```

```python
import functools
import math

import jax
import jax.numpy as jnp
from jax import lax
from jax.experimental import pallas as pl
from jax.experimental.pallas import tpu as pltpu
from jax.sharding import PartitionSpec as P

MESH = pl.DeviceIdType.MESH
F32 = jnp.float32
BF16 = jnp.bfloat16
CORES = 2
CHIPS = 4
MEMBERS = CHIPS * CORES
OUT_ROWS = 6
SLOTS = 32
SCALE = 4.0 * math.log2(math.e)


class Square:
    Q, R = 8, 8

    @staticmethod
    def split(dp, sub):
        z, x, y, core = dp // 4, dp % 4, sub // 2, sub % 2
        return (z % 2) * 2 + y % 2, core, x * 2 + y // 2, z // 2

    @staticmethod
    def join(chip, core, q, r):
        z, x, y = r * 2 + chip // 2, q // 2, (q % 2) * 2 + chip % 2
        return z * 4 + x, y * 2 + core


class Line:
    Q, R = 16, 4

    @staticmethod
    def split(dp, sub):
        z, x, y, core = dp // 4, dp % 4, sub // 2, sub % 2
        return z % 4, core, x * 4 + y, z // 4

    @staticmethod
    def join(chip, core, q, r):
        return (r * 4 + chip) * 4 + q // 4, (q % 4) * 2 + core


class Column:
    Q, R = 4, 16

    @staticmethod
    def split(dp, sub):
        return sub // 2, sub % 2, dp % 4, dp // 4

    @staticmethod
    def join(chip, core, q, r):
        return r * 4 + q, chip * 2 + core


LAYOUT = Square


def iota(shape, dim):
    return lax.broadcasted_iota(jnp.int32, shape, dim)


def kernel(lay, pts_in, cand, owner, out_cent, out_mass, out_min,
           pts, pack, packs, target, dense, psum, rsend, rrecv, asend, arecv, csend, crecv,
           c_buf, cn_buf, pn_buf, acc, mass, minsend, minrecv, fsend, frecv, fsum, gsend, grecv,
           s_pack, r_pack, s_pts, r_pts, s_sib, r_sib, s_d, r_d, s_r, r_r, s_a, r_a, s_c, r_c,
           s_f, r_f, s_g, r_g, s_m, r_m):
    Q, R = lay.Q, lay.R
    per_q = R * OUT_ROWS
    rows = Q * per_q
    n_pts = pts_in.shape[0]
    rounds, per_round = cand.shape
    dp, sub = lax.axis_index("dp"), lax.axis_index("sub")
    chip, core, q_me, r_me = lay.split(dp, sub)
    member = chip * CORES + core
    device = dp * MEMBERS + sub

    def to_member(m):
        return lay.join(m // CORES, m % CORES, q_me, r_me)

    def to_plane(q):
        return lay.join(chip, core, q, r_me)

    def to_ring(r):
        return lay.join(chip, core, q_me, r)

    def copy(src, dst, send, recv, where):
        return pltpu.make_async_remote_copy(
            src_ref=src, dst_ref=dst, send_sem=send, recv_sem=recv, device_id=where, device_id_type=MESH)

    def peers(n, me):
        def wrap(body):
            def step(i, carry):
                body(lax.rem(me + i, n))
                return carry
            lax.fori_loop(1, n, step, 0)
        return wrap

    barrier = pltpu.get_barrier_semaphore()
    for n, me, to in ((MEMBERS, member, to_member), (Q, q_me, to_plane), (R, r_me, to_ring)):
        @peers(n, me)
        def _(p, to=to):
            pl.semaphore_signal(barrier, inc=1, device_id=to(p), device_id_type=MESH)

    local = iota((n_pts, 128), 0) + device * n_pts
    tiles = per_round // 128
    hit = jnp.zeros((n_pts, 128), F32)
    for rnd in range(rounds):
        for t in range(tiles):
            hit = jnp.where(local == cand[rnd:rnd + 1, 128 * t:128 * (t + 1)], 1.0, hit)
    hit = jnp.max(hit, axis=1, keepdims=True)
    below = jnp.where(iota((n_pts, n_pts), 1) < iota((n_pts, n_pts), 0), 1.0, 0.0).astype(BF16)
    rank = jnp.dot(below, jnp.broadcast_to(hit, (n_pts, 128)).astype(BF16), preferred_element_type=F32)
    lane = iota((n_pts, 128), 1)
    rank = rank.astype(jnp.int32)
    sel = jnp.where((rank == lane) & (lane < SLOTS), hit, 0.0).astype(BF16)
    picked = lax.dot_general(sel, pts_in[...], (((0,), (0,)), ((), ())), preferred_element_type=F32)
    shift = (member % 4) * SLOTS
    moved = jnp.where(rank + shift == lane, hit, 0.0)
    rowno = iota((n_pts, 128), 0)
    high = jnp.sum(moved * (rowno // 2).astype(F32), axis=0, keepdims=True)
    low = jnp.sum(moved * (rowno % 2).astype(F32), axis=0, keepdims=True)
    used = jnp.sum(moved, axis=0, keepdims=True)
    which = iota((16, 128), 0)
    ids = jnp.where(which == 0, high, jnp.where(which == 1, low, jnp.where(which == 2, used, 0.0)))
    pack[0:SLOTS, :] = picked[0:SLOTS, 0:128].astype(BF16)
    pack[SLOTS:2 * SLOTS, :] = picked[0:SLOTS, 128:256].astype(BF16)
    pack[2 * SLOTS:2 * SLOTS + 16, :] = ids.astype(BF16)
    packs[member] = pack[...]
    pts[member] = pts_in[...]

    pl.semaphore_wait(barrier, MEMBERS + Q + R - 3)

    @peers(MEMBERS, member)
    def _(p):
        copy(pack, packs.at[member], s_pack.at[p], r_pack.at[member], to_member(p)).start()

    @peers(CHIPS, chip)
    def _(p):
        copy(pts_in, pts.at[member], s_pts.at[p], r_pts.at[chip], lay.join(p, core, q_me, r_me)).start()

    sibling = lay.join(chip, 1 - core, q_me, r_me)
    copy(pts_in, pts.at[member], s_sib.at[chip], r_sib.at[chip], sibling).start()

    for blk in range(rows // 128):
        i = iota((128, 128), 0) + 128 * blk
        group = (i * 10923) // 65536
        qq, rr, jj = group // R, group % R, i - group * OUT_ROWS
        ddp, dsub = lay.join(chip, core, qq, rr)
        slot = (ddp * MEMBERS + dsub) * OUT_ROWS + jj
        found = jnp.zeros((128, 128), F32)
        for rnd in range(rounds):
            for t in range(tiles):
                c = cand[rnd:rnd + 1, 128 * t:128 * (t + 1)].astype(F32)
                o = owner[rnd * tiles + t:rnd * tiles + t + 1, :]
                found = jnp.where(slot == o, c, found)
        target[128 * blk:128 * (blk + 1), :] = jnp.broadcast_to(
            jnp.sum(found, axis=1, keepdims=True), (128, 128))

    @peers(MEMBERS, member)
    def _(p):
        copy(pack, packs.at[p], s_pack.at[p], r_pack.at[p], to_member(p)).wait_recv()

    hots = []
    for half in range(2):
        ident = jnp.zeros((1, 128), F32)
        for m in range(4 * half, 4 * half + 4):
            mdp, msub = to_member(m)
            tile = packs[m, 2 * SLOTS:2 * SLOTS + 16, :].astype(F32)
            first = ((mdp * MEMBERS + msub) * n_pts + 1).astype(F32)
            ident = ident + 2.0 * tile[0:1, :] + tile[1:2, :] + first * tile[2:3, :]
        hots.append(jnp.where(target[...] + 1.0 == ident, 1.0, 0.0).astype(BF16))
    hot = jnp.concatenate(hots, axis=1)
    left = jnp.dot(hot, packs[:, 0:SLOTS, :].reshape(MEMBERS * SLOTS, 128), preferred_element_type=F32)
    right = jnp.dot(hot, packs[:, SLOTS:2 * SLOTS, :].reshape(MEMBERS * SLOTS, 128), preferred_element_type=F32)
    for q in range(Q):
        both = jnp.concatenate([left[per_q * q:per_q * (q + 1)], right[per_q * q:per_q * (q + 1)]], axis=0)
        dense[q] = both.astype(BF16)

    @peers(Q, q_me)
    def _(p):
        copy(dense.at[p], crecv.at[q_me], s_d.at[p], r_d.at[q_me], to_plane(p)).start()

    psum[...] = dense[q_me].astype(F32)

    @peers(Q, q_me)
    def _(p):
        copy(dense.at[p], crecv.at[p], s_d.at[p], r_d.at[p], to_plane(p)).wait_recv()
        psum[...] += crecv[p].astype(F32)

    for r in range(R):
        a = psum[OUT_ROWS * r:OUT_ROWS * (r + 1), :]
        b = psum[per_q + OUT_ROWS * r:per_q + OUT_ROWS * (r + 1), :]
        pad = jnp.zeros((2, 128), F32)
        rsend[r] = jnp.concatenate([a, pad, b, pad], axis=0).astype(BF16)

    @peers(R, r_me)
    def _(p):
        copy(rsend.at[p], rrecv.at[r_me], s_r.at[p], r_r.at[r_me], to_ring(p)).start()

    gsend[0] = rsend[r_me].astype(F32)

    @peers(R, r_me)
    def _(p):
        copy(rsend.at[p], rrecv.at[p], s_r.at[p], r_r.at[p], to_ring(p)).wait_recv()
        gsend[0] += rrecv[p].astype(F32)

    asend[...] = gsend[0].astype(BF16)
    arecv[r_me] = asend[...]

    @peers(R, r_me)
    def _(p):
        copy(asend, arecv.at[r_me], s_a.at[p], r_a.at[r_me], to_ring(p)).start()

    @peers(R, r_me)
    def _(p):
        copy(asend, arecv.at[p], s_a.at[p], r_a.at[p], to_ring(p)).wait_recv()

    for r in range(R):
        tile = arecv[r].astype(F32)
        psum[OUT_ROWS * r:OUT_ROWS * (r + 1), :] = tile[0:OUT_ROWS, :]
        psum[per_q + OUT_ROWS * r:per_q + OUT_ROWS * (r + 1), :] = tile[8:8 + OUT_ROWS, :]
    csend[...] = psum[...].astype(BF16)

    @peers(Q, q_me)
    def _(p):
        copy(csend, c_buf.at[q_me], s_c.at[p], r_c.at[q_me], to_plane(p)).start()

    c_buf[q_me] = csend[...]

    @peers(CHIPS, chip)
    def _(p):
        slot = pts.at[p * CORES + core]
        copy(pts_in, slot, s_pts.at[p], r_pts.at[p], lay.join(p, core, q_me, r_me)).wait_recv()
        copy(slot, slot, s_sib.at[p], r_sib.at[p], sibling).start()

    @peers(Q, q_me)
    def _(p):
        copy(csend, c_buf.at[p], s_c.at[p], r_c.at[p], to_plane(p)).wait_recv()

    lefts = jnp.concatenate([c_buf[q, 0:per_q, :].astype(F32) for q in range(Q)], axis=0)
    rights = jnp.concatenate([c_buf[q, per_q:2 * per_q, :].astype(F32) for q in range(Q)], axis=0)
    chosen = jnp.concatenate([lefts, rights], axis=1)
    cn_buf[...] = jnp.broadcast_to(jnp.sum(chosen * chosen, axis=1, keepdims=True), (rows, 128))
    pn_buf[...] = (2.0 * chosen).astype(BF16)
    acc[...] = jnp.zeros_like(acc)
    mass[...] = jnp.zeros_like(mass)

    def block(idx):
        part = pts[idx]
        wide = part.astype(F32)
        square = wide * wide
        top = square.astype(BF16)
        rest = (square - top.astype(F32)).astype(BF16)
        ones = jnp.ones((8, part.shape[1]), BF16)
        nt = (((1,), (1,)), ((), ()))
        pn = (lax.dot_general(ones, top, nt, preferred_element_type=F32)
              + lax.dot_general(ones, rest, nt, preferred_element_type=F32))[0:1, :]
        dots = lax.dot_general(pn_buf[...], part, nt, preferred_element_type=F32)
        less = dots - cn_buf[:, 0:1]
        near = pn - jnp.max(less, axis=0, keepdims=True)
        weight = jnp.exp2((less - pn) * SCALE).astype(BF16)
        acc[...] += jnp.dot(weight, part, preferred_element_type=F32)
        wide_w = weight.astype(F32)
        m = wide_w[:, 0:128]
        for t in range(1, n_pts // 128):
            m = m + wide_w[:, 128 * t:128 * (t + 1)]
        mass[...] += m
        for t in range(n_pts // 128):
            minsend[idx, t:t + 1, :] = near[:, 128 * t:128 * (t + 1)]

    def same_core(i, carry):
        block(lax.rem(chip + i, CHIPS) * CORES + core)
        return carry

    def other_core(i, carry):
        p = lax.rem(chip + i, CHIPS)
        slot = pts.at[p * CORES + 1 - core]
        copy(slot, slot, s_sib.at[p], r_sib.at[p], sibling).wait_recv()
        block(p * CORES + 1 - core)
        return carry

    lax.fori_loop(0, CHIPS, same_core, 0)
    lax.fori_loop(0, CHIPS, other_core, 0)

    total = jnp.sum(mass[...], axis=1, keepdims=True)
    diag = iota((per_q, 128), 0) == iota((per_q, 128), 1)
    for q in range(Q):
        lo, hi = per_q * q, per_q * (q + 1)
        fsend[q, 0:per_q, :] = acc[lo:hi, 0:128]
        fsend[q, per_q:2 * per_q, :] = acc[lo:hi, 128:256]
        line = jnp.sum(jnp.where(diag, total[lo:hi], 0.0), axis=0, keepdims=True)
        fsend[q, 2 * per_q:2 * per_q + 8, :] = jnp.broadcast_to(line, (8, 128))

    @peers(Q, q_me)
    def _(p):
        copy(fsend.at[p], frecv.at[q_me], s_f.at[p], r_f.at[q_me], to_plane(p)).start()

    @peers(MEMBERS, member)
    def _(p):
        copy(minsend.at[p], minrecv.at[member], s_m.at[p], r_m.at[member], to_member(p)).start()

    fsum[...] = fsend[q_me]

    @peers(Q, q_me)
    def _(p):
        copy(fsend.at[p], frecv.at[p], s_f.at[p], r_f.at[p], to_plane(p)).wait_recv()
        fsum[...] += frecv[p]

    for r in range(R):
        lo, hi = OUT_ROWS * r, OUT_ROWS * (r + 1)
        gsend[r, 0:OUT_ROWS, :] = fsum[lo:hi, :]
        gsend[r, OUT_ROWS:8, :] = fsum[2 * per_q:2 * per_q + 8 - OUT_ROWS, :]
        gsend[r, 8:8 + OUT_ROWS, :] = fsum[per_q + lo:per_q + hi, :]
        gsend[r, 8 + OUT_ROWS:16, :] = jnp.zeros((8 - OUT_ROWS, 128), F32)

    @peers(R, r_me)
    def _(p):
        copy(gsend.at[p], grecv.at[r_me], s_g.at[p], r_g.at[r_me], to_ring(p)).start()

    out_min[...] = minsend[member]

    @peers(MEMBERS, member)
    def _(p):
        copy(minsend.at[p], minrecv.at[p], s_m.at[p], r_m.at[p], to_member(p)).wait_recv()
        out_min[...] = jnp.minimum(out_min[...], minrecv[p])

    final = fsum.at[0:16]
    final[...] = gsend[r_me]

    @peers(R, r_me)
    def _(p):
        copy(gsend.at[p], grecv.at[p], s_g.at[p], r_g.at[p], to_ring(p)).wait_recv()
        final[...] += grecv[p]

    both = final[...]
    line = both[OUT_ROWS:OUT_ROWS + 1, :]
    pick = iota((8, 128), 1) == iota((8, 128), 0) + OUT_ROWS * r_me
    column = jnp.sum(jnp.where(pick, line, 0.0), axis=1, keepdims=True)
    out_cent[:, 0:128] = both[0:OUT_ROWS, :] / column[0:OUT_ROWS]
    out_cent[:, 128:256] = both[8:8 + OUT_ROWS, :] / column[0:OUT_ROWS]
    eye = iota((8, 128), 1) == iota((8, 128), 0)
    out_mass[...] = jnp.sum(jnp.where(eye, column, 0.0), axis=0, keepdims=True)

    @peers(MEMBERS, member)
    def _(p):
        copy(pack, packs.at[member], s_pack.at[p], r_pack.at[p], to_member(p)).wait_send()
        copy(minsend.at[p], minrecv.at[p], s_m.at[p], r_m.at[p], to_member(p)).wait_send()

    @peers(CHIPS, chip)
    def _(p):
        slot = pts.at[p * CORES + core]
        copy(pts_in, slot, s_pts.at[p], r_pts.at[p], sibling).wait_send()
        copy(slot, slot, s_sib.at[p], r_sib.at[p], sibling).wait_send()

    copy(pts_in, pts.at[member], s_sib.at[chip], r_sib.at[chip], sibling).wait_send()

    @peers(Q, q_me)
    def _(p):
        copy(dense.at[p], crecv.at[p], s_d.at[p], r_d.at[p], sibling).wait_send()
        copy(csend, c_buf.at[p], s_c.at[p], r_c.at[p], sibling).wait_send()
        copy(fsend.at[p], frecv.at[p], s_f.at[p], r_f.at[p], sibling).wait_send()

    @peers(R, r_me)
    def _(p):
        copy(rsend.at[p], rrecv.at[p], s_r.at[p], r_r.at[p], sibling).wait_send()
        copy(asend, arecv.at[p], s_a.at[p], r_a.at[p], sibling).wait_send()
        copy(gsend.at[p], grecv.at[p], s_g.at[p], r_g.at[p], sibling).wait_send()


def on_device(lay, points, candidates, owner_slot):
    Q, R = lay.Q, lay.R
    n_pts, dim = points.shape
    per_q = R * OUT_ROWS
    rows = Q * per_q
    owner = owner_slot.reshape(-1, 128)
    vmem = pltpu.VMEM
    dma = pltpu.SemaphoreType.DMA
    scratch = [
        vmem((MEMBERS, n_pts, dim), BF16),
        vmem((2 * SLOTS + 16, 128), BF16),
        vmem((MEMBERS, 2 * SLOTS + 16, 128), BF16),
        vmem((rows, 128), F32),
        vmem((Q, 2 * per_q, 128), BF16),
        vmem((2 * per_q, 128), F32),
        vmem((R, 16, 128), BF16),
        vmem((R, 16, 128), BF16),
        vmem((16, 128), BF16),
        vmem((R, 16, 128), BF16),
        vmem((2 * per_q, 128), BF16),
        vmem((Q, 2 * per_q, 128), BF16),
        vmem((Q, 2 * per_q, 128), BF16),
        vmem((rows, 128), F32),
        vmem((rows, dim), BF16),
        vmem((rows, dim), F32),
        vmem((rows, 128), F32),
        vmem((MEMBERS, n_pts // 128, 128), F32),
        vmem((MEMBERS, n_pts // 128, 128), F32),
        vmem((Q, 2 * per_q + 8, 128), F32),
        vmem((Q, 2 * per_q + 8, 128), F32),
        vmem((2 * per_q + 8, 128), F32),
        vmem((R, 16, 128), F32),
        vmem((R, 16, 128), F32),
    ]
    for n in (MEMBERS, CHIPS, CHIPS, Q, R, R, Q, Q, R, MEMBERS):
        scratch += [dma((n,)), dma((n,))]
    cent, mass, near = pl.pallas_call(
        functools.partial(kernel, lay),
        out_shape=(
            jax.ShapeDtypeStruct((OUT_ROWS, dim), F32),
            jax.ShapeDtypeStruct((1, 128), F32),
            jax.ShapeDtypeStruct((n_pts // 128, 128), F32),
        ),
        in_specs=[pl.BlockSpec(memory_space=vmem)] * 3,
        out_specs=[pl.BlockSpec(memory_space=vmem)] * 3,
        scratch_shapes=scratch,
        compiler_params=pltpu.CompilerParams(
            collective_id=0, has_side_effects=True, vmem_limit_bytes=48 * 2 ** 20),
    )(points, candidates, owner)
    return cent, mass[0, 0:OUT_ROWS], near.reshape(-1)


def solution(mesh):
    return jax.shard_map(
        functools.partial(on_device, LAYOUT),
        mesh=mesh,
        in_specs=(P(("dp", "sub"), None), P(), P()),
        out_specs=(P(("dp", "sub"), None), P(("dp", "sub")), P(("dp", "sub"))),
        check_vma=False,
    )
```

```python
import math

import jax
import jax.numpy as jnp
from jax import lax
from jax.experimental import pallas as pl
from jax.experimental.pallas import tpu as pltpu
from jax.sharding import PartitionSpec as P

MESH = pl.DeviceIdType.MESH
F32 = jnp.float32
BF16 = jnp.bfloat16
CORES = 2
CHIPS = 4
MEMBERS = CHIPS * CORES
OUT_ROWS = 6
SLOTS = 32
SCALE = 4.0 * math.log2(math.e)


Q, R = 16, 4
X, Z = 4, 16


def iota(shape, dim):
    return lax.broadcasted_iota(jnp.int32, shape, dim)


def kernel(pts_hbm, cand_hbm, owner_hbm, out_cent, out_mass, out_min,
           pts, cand, owner, pack, packs, target, dense, drecv, psum, rsend, rrecv, csend, c_buf,
           cn_buf, c_twice, acc, mass, minsend, minrecv, fsend, frecv, fsum, gsend, grecv,
           s_in, s_pack, r_pack, s_pts, r_pts, s_sib, r_sib, s_d, r_d, s_r, r_r, s_c, r_c,
           s_f, r_f, s_g, r_g, s_m, r_m):
    per_q = R * OUT_ROWS
    per_x = Z * OUT_ROWS
    rows = Q * per_q
    n_pts = pts_hbm.shape[0]
    rounds, per_round = cand.shape
    tiles = per_round // 128
    dp, sub = lax.axis_index("dp"), lax.axis_index("sub")
    z, x, chip, core = dp // X, dp % X, sub // CORES, sub % CORES
    low, high = z % 4, z // 4
    q_me = x * 4 + low
    k_me = low * R + high
    device = dp * MEMBERS + sub
    sibling = (dp, chip * CORES + 1 - core)

    def to_member(m):
        return dp, m

    def to_chip(p):
        return dp, p * CORES + core

    def to_plane(q):
        return (high * 4 + q % 4) * X + q // 4, sub

    def to_ring(r):
        return (r * 4 + low) * X + x, sub

    def to_x(p):
        return z * X + p, sub

    def to_z(p):
        return p * X + x, sub

    def z_slot(p):
        return (p % 4) * R + p // 4

    def copy(src, dst, send, recv, where):
        return pltpu.make_async_remote_copy(
            src_ref=src, dst_ref=dst, send_sem=send, recv_sem=recv, device_id=where, device_id_type=MESH)

    def peers(n, me):
        def wrap(body):
            def step(i, carry):
                body(lax.rem(me + i, n))
                return carry
            lax.fori_loop(1, n, step, 0)
        return wrap

    def far_first(n, me):
        def wrap(body):
            def step(i, carry):
                body(lax.rem(me + n // 2 + (1 - 2 * (i % 2)) * ((i + 1) // 2), n))
                return carry
            lax.fori_loop(0, n - 1, step, 0)
        return wrap

    barrier = pltpu.get_barrier_semaphore()
    for order, n, me, to in ((far_first, Z, z, to_z), (peers, Q, q_me, to_plane), (peers, MEMBERS, sub, to_member)):
        @order(n, me)
        def _(p, to=to):
            pl.semaphore_signal(barrier, inc=1, device_id=to(p), device_id_type=MESH)

    loads = [
        pltpu.make_async_copy(cand_hbm, cand, s_in.at[0]),
        pltpu.make_async_copy(pts_hbm, pts.at[sub], s_in.at[1]),
        pltpu.make_async_copy(owner_hbm, owner, s_in.at[2]),
    ]
    for load in loads:
        load.start()
    for load in loads:
        load.wait()

    step = 64
    hits = []
    for lo in range(0, n_pts, step):
        local = iota((step, 128), 0) + (device * n_pts + lo)
        hit = jnp.zeros((step, 128), F32)
        for rnd in range(rounds):
            for t in range(tiles):
                hit = jnp.where(local == cand[rnd:rnd + 1, 128 * t:128 * (t + 1)], 1.0, hit)
        hits.append(jnp.max(hit, axis=1, keepdims=True))
    hit = jnp.concatenate(hits, axis=0)
    below = jnp.where(iota((n_pts, n_pts), 1) < iota((n_pts, n_pts), 0), 1.0, 0.0).astype(BF16)
    rank = jnp.dot(below, jnp.broadcast_to(hit, (n_pts, 128)).astype(BF16), preferred_element_type=F32)
    rank = rank.astype(jnp.int32)
    lane = iota((n_pts, 128), 1)
    sel = jnp.where((rank == lane) & (lane < SLOTS), hit, 0.0).astype(BF16)
    picked = lax.dot_general(sel, pts[sub], (((0,), (0,)), ((), ())), preferred_element_type=F32)
    moved = jnp.where(rank + (sub % 4) * SLOTS == lane, hit, 0.0)
    rowno = iota((n_pts, 128), 0)
    upper = jnp.sum(moved * (rowno >> 1).astype(F32), axis=0, keepdims=True)
    lower = jnp.sum(moved * (rowno & 1).astype(F32), axis=0, keepdims=True)
    used = jnp.sum(moved, axis=0, keepdims=True)
    which = iota((16, 128), 0)
    ids = jnp.where(which == 0, upper, jnp.where(which == 1, lower, jnp.where(which == 2, used, 0.0)))
    pack[0:SLOTS, :] = picked[0:SLOTS, 0:128].astype(BF16)
    pack[SLOTS:2 * SLOTS, :] = picked[0:SLOTS, 128:256].astype(BF16)
    pack[2 * SLOTS:2 * SLOTS + 16, :] = ids.astype(BF16)
    packs[sub] = pack[...]

    pl.semaphore_wait(barrier, MEMBERS + Q + Z - 3)

    @peers(MEMBERS, sub)
    def _(p):
        copy(pack, packs.at[sub], s_pack.at[p], r_pack.at[sub], to_member(p)).start()

    for blk in range(rows // 128):
        i = iota((128, 128), 0) + 128 * blk
        group = (i * 10923) >> 16
        q, r, j = group >> 2, group & 3, i - group * OUT_ROWS
        slot = ((((r << 2) + (q & 3)) * X + (q >> 2)) * MEMBERS + sub) * OUT_ROWS + j
        found = jnp.zeros((128, 128), F32)
        for rnd in range(rounds):
            for t in range(tiles):
                c = cand[rnd:rnd + 1, 128 * t:128 * (t + 1)].astype(F32)
                o = owner[rnd * tiles + t:rnd * tiles + t + 1, :]
                found = jnp.where(slot == o, c, found)
        target[128 * blk:128 * (blk + 1), :] = jnp.broadcast_to(
            jnp.sum(found, axis=1, keepdims=True), (128, 128))

    @peers(MEMBERS, sub)
    def _(p):
        copy(pack, packs.at[p], s_pack.at[p], r_pack.at[p], to_member(p)).wait_recv()

    hots = []
    for half in range(2):
        ident = jnp.zeros((1, 128), F32)
        for m in range(4 * half, 4 * half + 4):
            tile = packs[m, 2 * SLOTS:2 * SLOTS + 16, :].astype(F32)
            first = ((dp * MEMBERS + m) * n_pts + 1).astype(F32)
            ident = ident + 2.0 * tile[0:1, :] + tile[1:2, :] + first * tile[2:3, :]
        hots.append(jnp.where(target[...] + 1.0 == ident, 1.0, 0.0).astype(BF16))
    hot = jnp.concatenate(hots, axis=1)
    left = jnp.dot(hot, packs[:, 0:SLOTS, :].reshape(MEMBERS * SLOTS, 128), preferred_element_type=F32)
    right = jnp.dot(hot, packs[:, SLOTS:2 * SLOTS, :].reshape(MEMBERS * SLOTS, 128), preferred_element_type=F32)
    for q in range(Q):
        both = jnp.concatenate([left[per_q * q:per_q * (q + 1)], right[per_q * q:per_q * (q + 1)]], axis=0)
        dense[q] = both.astype(BF16)

    @far_first(Q, q_me)
    def _(p):
        copy(dense.at[p], drecv.at[q_me], s_d.at[p], r_d.at[q_me], to_plane(p)).start()

    @peers(CHIPS, chip)
    def _(p):
        copy(pts.at[sub], pts.at[sub], s_pts.at[p], r_pts.at[chip], to_chip(p)).start()

    copy(pts.at[sub], pts.at[sub], s_sib.at[chip], r_sib.at[chip], sibling).start()

    psum[...] = dense[q_me].astype(F32)

    @far_first(Q, q_me)
    def _(p):
        copy(dense.at[p], drecv.at[p], s_d.at[p], r_d.at[p], to_plane(p)).wait_recv()
        psum[...] += drecv[p].astype(F32)

    rsend[...] = psum[...].astype(BF16)

    @far_first(R, high)
    def _(p):
        copy(rsend, rrecv.at[high], s_r.at[p], r_r.at[high], to_ring(p)).start()

    @far_first(R, high)
    def _(p):
        copy(rsend, rrecv.at[p], s_r.at[p], r_r.at[p], to_ring(p)).wait_recv()
        psum[...] += rrecv[p].astype(F32)

    csend[...] = psum[...].astype(BF16)

    @far_first(Q, q_me)
    def _(p):
        copy(csend, c_buf.at[q_me], s_c.at[p], r_c.at[q_me], to_plane(p)).start()

    c_buf[q_me] = csend[...]

    @peers(CHIPS, chip)
    def _(p):
        slot = pts.at[p * CORES + core]
        copy(slot, slot, s_pts.at[p], r_pts.at[p], to_chip(p)).wait_recv()
        copy(slot, slot, s_sib.at[p], r_sib.at[p], sibling).start()

    @far_first(Q, q_me)
    def _(p):
        copy(csend, c_buf.at[p], s_c.at[p], r_c.at[p], to_plane(p)).wait_recv()

    lefts = jnp.concatenate([c_buf[q, 0:per_q, :].astype(F32) for q in range(Q)], axis=0)
    rights = jnp.concatenate([c_buf[q, per_q:2 * per_q, :].astype(F32) for q in range(Q)], axis=0)
    chosen = jnp.concatenate([lefts, rights], axis=1)
    cn_buf[...] = jnp.broadcast_to(jnp.sum(chosen * chosen, axis=1, keepdims=True), (rows, 128))
    c_twice[...] = (2.0 * chosen).astype(BF16)
    acc[...] = jnp.zeros_like(acc)
    mass[...] = jnp.zeros_like(mass)

    def block(idx):
        part = pts[idx]
        wide = part.astype(F32)
        square = wide * wide
        top = square.astype(BF16)
        rest = (square - top.astype(F32)).astype(BF16)
        ones = jnp.ones((8, part.shape[1]), BF16)
        nt = (((1,), (1,)), ((), ()))
        pn = (lax.dot_general(ones, top, nt, preferred_element_type=F32)
              + lax.dot_general(ones, rest, nt, preferred_element_type=F32))[0:1, :]
        dots = lax.dot_general(c_twice[...], part, nt, preferred_element_type=F32)
        less = dots - cn_buf[:, 0:1]
        near = pn - jnp.max(less, axis=0, keepdims=True)
        weight = jnp.exp2((less - pn) * SCALE).astype(BF16)
        acc[...] += jnp.dot(weight, part, preferred_element_type=F32)
        wide_w = weight.astype(F32)
        m = wide_w[:, 0:128]
        for t in range(1, n_pts // 128):
            m = m + wide_w[:, 128 * t:128 * (t + 1)]
        mass[...] += m
        for t in range(n_pts // 128):
            minsend[idx, t:t + 1, :] = near[:, 128 * t:128 * (t + 1)]

    def same_core(i, carry):
        block(lax.rem(chip + i, CHIPS) * CORES + core)
        return carry

    def other_core(i, carry):
        p = lax.rem(chip + i, CHIPS)
        slot = pts.at[p * CORES + 1 - core]
        copy(slot, slot, s_sib.at[p], r_sib.at[p], sibling).wait_recv()
        block(p * CORES + 1 - core)
        return carry

    lax.fori_loop(0, CHIPS, same_core, 0)
    lax.fori_loop(0, CHIPS, other_core, 0)

    total = jnp.sum(mass[...], axis=1, keepdims=True)
    diag = iota((per_x, 128), 0) == iota((per_x, 128), 1)
    for p in range(X):
        lo, hi = per_x * p, per_x * (p + 1)
        fsend[p, 0:per_x, :] = acc[lo:hi, 0:128]
        fsend[p, per_x:2 * per_x, :] = acc[lo:hi, 128:256]
        line = jnp.sum(jnp.where(diag, total[lo:hi], 0.0), axis=0, keepdims=True)
        fsend[p, 2 * per_x:2 * per_x + 8, :] = jnp.broadcast_to(line, (8, 128))

    @far_first(X, x)
    def _(p):
        copy(fsend.at[p], frecv.at[x], s_f.at[p], r_f.at[x], to_x(p)).start()

    @peers(MEMBERS, sub)
    def _(p):
        copy(minsend.at[p], minrecv.at[sub], s_m.at[p], r_m.at[sub], to_member(p)).start()

    fsum[...] = fsend[x]

    @far_first(X, x)
    def _(p):
        copy(fsend.at[p], frecv.at[p], s_f.at[p], r_f.at[p], to_x(p)).wait_recv()
        fsum[...] += frecv[p]

    for k in range(Z):
        lo, hi = OUT_ROWS * k, OUT_ROWS * (k + 1)
        gsend[k, 0:OUT_ROWS, :] = fsum[lo:hi, :]
        gsend[k, OUT_ROWS:8, :] = fsum[2 * per_x:2 * per_x + 8 - OUT_ROWS, :]
        gsend[k, 8:8 + OUT_ROWS, :] = fsum[per_x + lo:per_x + hi, :]
        gsend[k, 8 + OUT_ROWS:16, :] = jnp.zeros((8 - OUT_ROWS, 128), F32)

    @far_first(Z, z)
    def _(p):
        copy(gsend.at[z_slot(p)], grecv.at[z], s_g.at[p], r_g.at[z], to_z(p)).start()

    out_min[...] = minsend[sub]

    @peers(MEMBERS, sub)
    def _(p):
        copy(minsend.at[p], minrecv.at[p], s_m.at[p], r_m.at[p], to_member(p)).wait_recv()
        out_min[...] = jnp.minimum(out_min[...], minrecv[p])

    final = fsum.at[0:16]
    final[...] = gsend[k_me]

    @peers(Z, z)
    def _(p):
        copy(gsend.at[p], grecv.at[p], s_g.at[p], r_g.at[p], to_z(p)).wait_recv()
        final[...] += grecv[p]

    both = final[...]
    line = both[OUT_ROWS:OUT_ROWS + 1, :]
    pick = iota((8, 128), 1) == iota((8, 128), 0) + OUT_ROWS * k_me
    column = jnp.sum(jnp.where(pick, line, 0.0), axis=1, keepdims=True)
    out_cent[:, 0:128] = both[0:OUT_ROWS, :] / column[0:OUT_ROWS]
    out_cent[:, 128:256] = both[8:8 + OUT_ROWS, :] / column[0:OUT_ROWS]
    eye = iota((8, 128), 1) == iota((8, 128), 0)
    out_mass[...] = jnp.sum(jnp.where(eye, column, 0.0), axis=0, keepdims=True)

    @peers(MEMBERS, sub)
    def _(p):
        copy(pack, packs.at[sub], s_pack.at[p], r_pack.at[p], to_member(p)).wait_send()

    @peers(MEMBERS, sub)
    def _(p):
        copy(minsend.at[p], minrecv.at[p], s_m.at[p], r_m.at[p], to_member(p)).wait_send()

    @peers(CHIPS, chip)
    def _(p):
        slot = pts.at[p * CORES + core]
        copy(slot, slot, s_pts.at[p], r_pts.at[p], sibling).wait_send()
        copy(slot, slot, s_sib.at[p], r_sib.at[p], sibling).wait_send()

    copy(pts.at[sub], pts.at[sub], s_sib.at[chip], r_sib.at[chip], sibling).wait_send()

    @peers(Q, q_me)
    def _(p):
        copy(dense.at[p], drecv.at[p], s_d.at[p], r_d.at[p], sibling).wait_send()

    @peers(Q, q_me)
    def _(p):
        copy(csend, c_buf.at[p], s_c.at[p], r_c.at[p], sibling).wait_send()

    @peers(R, high)
    def _(p):
        copy(rsend, rrecv.at[p], s_r.at[p], r_r.at[p], sibling).wait_send()

    @peers(X, x)
    def _(p):
        copy(fsend.at[p], frecv.at[p], s_f.at[p], r_f.at[p], sibling).wait_send()

    @peers(Z, z)
    def _(p):
        copy(gsend.at[p], grecv.at[p], s_g.at[p], r_g.at[p], sibling).wait_send()


def on_device(points, candidates, owner_slot):
    n_pts, dim = points.shape
    per_q, per_x = R * OUT_ROWS, Z * OUT_ROWS
    rows = Q * per_q
    owner = owner_slot.reshape(-1, 128)
    vmem = pltpu.VMEM
    dma = pltpu.SemaphoreType.DMA
    scratch = [
        vmem((MEMBERS, n_pts, dim), BF16),
        vmem(candidates.shape, jnp.int32),
        vmem(owner.shape, jnp.int32),
        vmem((2 * SLOTS + 16, 128), BF16),
        vmem((MEMBERS, 2 * SLOTS + 16, 128), BF16),
        vmem((rows, 128), F32),
        vmem((Q, 2 * per_q, 128), BF16),
        vmem((Q, 2 * per_q, 128), BF16),
        vmem((2 * per_q, 128), F32),
        vmem((2 * per_q, 128), BF16),
        vmem((R, 2 * per_q, 128), BF16),
        vmem((2 * per_q, 128), BF16),
        vmem((Q, 2 * per_q, 128), BF16),
        vmem((rows, 128), F32),
        vmem((rows, dim), BF16),
        vmem((rows, dim), F32),
        vmem((rows, 128), F32),
        vmem((MEMBERS, n_pts // 128, 128), F32),
        vmem((MEMBERS, n_pts // 128, 128), F32),
        vmem((X, 2 * per_x + 8, 128), F32),
        vmem((X, 2 * per_x + 8, 128), F32),
        vmem((2 * per_x + 8, 128), F32),
        vmem((Z, 16, 128), F32),
        vmem((Z, 16, 128), F32),
        dma((3,)),
    ]
    for n in (MEMBERS, CHIPS, CHIPS, Q, R, Q, X, Z, MEMBERS):
        scratch += [dma((n,)), dma((n,))]
    cent, mass, near = pl.pallas_call(
        kernel,
        out_shape=(
            jax.ShapeDtypeStruct((OUT_ROWS, dim), F32),
            jax.ShapeDtypeStruct((1, 128), F32),
            jax.ShapeDtypeStruct((n_pts // 128, 128), F32),
        ),
        in_specs=[pl.BlockSpec(memory_space=pltpu.HBM)] * 3,
        out_specs=[pl.BlockSpec(memory_space=vmem)] * 3,
        scratch_shapes=scratch,
        compiler_params=pltpu.CompilerParams(
            collective_id=0, has_side_effects=True, vmem_limit_bytes=55213 * 2 ** 10),
    )(points, candidates, owner)
    return cent, mass[0, 0:OUT_ROWS], near.reshape(-1)


def solution(mesh):
    return jax.shard_map(
        on_device,
        mesh=mesh,
        in_specs=(P(("dp", "sub"), None), P(), P()),
        out_specs=(P(("dp", "sub"), None), P(("dp", "sub")), P(("dp", "sub"))),
        check_vma=False,
    )
```

```python
import math

import jax
import jax.numpy as jnp
from jax import lax
from jax.experimental import pallas as pl
from jax.experimental.pallas import tpu as pltpu
from jax.sharding import PartitionSpec as P

MESH = pl.DeviceIdType.MESH
F32 = jnp.float32
BF16 = jnp.bfloat16
CORES = 2
CHIPS = 4
MEMBERS = CHIPS * CORES
OUT_ROWS = 6
SLOTS = 32
SCALE = 4.0 * math.log2(math.e)


Q, R = 16, 4
X, Z = 4, 16


def iota(shape, dim):
    return lax.broadcasted_iota(jnp.int32, shape, dim)


def kernel(pts_hbm, cand_hbm, owner_hbm, out_cent, out_mass, out_min,
           pts, cand, owner, pack, packs, target, dense, drecv, psum, rsend, rrecv, csend, c_buf,
           pn_buf, minsend, minrecv, fsend, frecv, fsum, gsend, grecv,
           s_in, s_pack, r_pack, s_pts, r_pts, s_sib, r_sib, s_d, r_d, s_r, r_r, s_c, r_c,
           s_f, r_f, s_g, r_g, s_m, r_m):
    per_q = R * OUT_ROWS
    per_x = Z * OUT_ROWS
    rows = Q * per_q
    n_pts = pts_hbm.shape[0]
    rounds, per_round = cand.shape
    tiles = per_round // 128
    dp, sub = lax.axis_index("dp"), lax.axis_index("sub")
    z, x, chip, core = dp // X, dp % X, sub // CORES, sub % CORES
    low, high = z % 4, z // 4
    q_me = x * 4 + low
    k_me = low * R + high
    device = dp * MEMBERS + sub
    sibling = (dp, chip * CORES + 1 - core)

    def to_member(m):
        return dp, m

    def to_chip(p):
        return dp, p * CORES + core

    def to_plane(q):
        return (high * 4 + q % 4) * X + q // 4, sub

    def to_ring(r):
        return (r * 4 + low) * X + x, sub

    def to_x(p):
        return z * X + p, sub

    def to_z(p):
        return p * X + x, sub

    def z_slot(p):
        return (p % 4) * R + p // 4

    def copy(src, dst, send, recv, where):
        return pltpu.make_async_remote_copy(
            src_ref=src, dst_ref=dst, send_sem=send, recv_sem=recv, device_id=where, device_id_type=MESH)

    def peers(n, me):
        def wrap(body):
            def step(i, carry):
                body(lax.rem(me + i, n))
                return carry
            lax.fori_loop(1, n, step, 0)
        return wrap

    def far_first(n, me):
        def wrap(body):
            def step(i, carry):
                body(lax.rem(me + n // 2 + (1 - 2 * (i % 2)) * ((i + 1) // 2), n))
                return carry
            lax.fori_loop(0, n - 1, step, 0)
        return wrap

    barrier = pltpu.get_barrier_semaphore()
    for order, n, me, to in ((far_first, Z, z, to_z), (peers, Q, q_me, to_plane), (peers, MEMBERS, sub, to_member)):
        @order(n, me)
        def _(p, to=to):
            pl.semaphore_signal(barrier, inc=1, device_id=to(p), device_id_type=MESH)

    loads = [
        pltpu.make_async_copy(cand_hbm, cand, s_in.at[0]),
        pltpu.make_async_copy(pts_hbm, pts.at[sub], s_in.at[1]),
        pltpu.make_async_copy(owner_hbm, owner, s_in.at[2]),
    ]
    for load in loads:
        load.start()
    for load in loads:
        load.wait()

    step = 64
    hits = []
    for lo in range(0, n_pts, step):
        local = iota((step, 128), 0) + (device * n_pts + lo)
        hit = jnp.zeros((step, 128), F32)
        for rnd in range(rounds):
            for t in range(tiles):
                hit = jnp.where(local == cand[rnd:rnd + 1, 128 * t:128 * (t + 1)], 1.0, hit)
        hits.append(jnp.max(hit, axis=1, keepdims=True))
    hit = jnp.concatenate(hits, axis=0)
    below = jnp.where(iota((n_pts, n_pts), 1) < iota((n_pts, n_pts), 0), 1.0, 0.0).astype(BF16)
    rank = jnp.dot(below, jnp.broadcast_to(hit, (n_pts, 128)).astype(BF16), preferred_element_type=F32)
    rank = rank.astype(jnp.int32)
    lane = iota((n_pts, 128), 1)
    sel = jnp.where((rank == lane) & (lane < SLOTS), hit, 0.0).astype(BF16)
    picked = lax.dot_general(sel, pts[sub], (((0,), (0,)), ((), ())), preferred_element_type=F32)
    moved = jnp.where(rank + (sub % 4) * SLOTS == lane, hit, 0.0)
    rowno = iota((n_pts, 128), 0)
    upper = jnp.sum(moved * (rowno >> 1).astype(F32), axis=0, keepdims=True)
    lower = jnp.sum(moved * (rowno & 1).astype(F32), axis=0, keepdims=True)
    used = jnp.sum(moved, axis=0, keepdims=True)
    which = iota((16, 128), 0)
    ids = jnp.where(which == 0, upper, jnp.where(which == 1, lower, jnp.where(which == 2, used, 0.0)))
    pack[0:SLOTS, :] = picked[0:SLOTS, 0:128].astype(BF16)
    pack[SLOTS:2 * SLOTS, :] = picked[0:SLOTS, 128:256].astype(BF16)
    pack[2 * SLOTS:2 * SLOTS + 16, :] = ids.astype(BF16)
    packs[sub] = pack[...]

    pl.semaphore_wait(barrier, MEMBERS + Q + Z - 3)

    @peers(MEMBERS, sub)
    def _(p):
        copy(pack, packs.at[sub], s_pack.at[p], r_pack.at[sub], to_member(p)).start()

    for blk in range(rows // 128):
        i = iota((128, 128), 0) + 128 * blk
        group = (i * 10923) >> 16
        q, r, j = group >> 2, group & 3, i - group * OUT_ROWS
        slot = ((((r << 2) + (q & 3)) * X + (q >> 2)) * MEMBERS + sub) * OUT_ROWS + j
        found = jnp.zeros((128, 128), F32)
        for rnd in range(rounds):
            for t in range(tiles):
                c = cand[rnd:rnd + 1, 128 * t:128 * (t + 1)].astype(F32)
                o = owner[rnd * tiles + t:rnd * tiles + t + 1, :]
                found = jnp.where(slot == o, c, found)
        target[128 * blk:128 * (blk + 1), :] = jnp.broadcast_to(
            jnp.sum(found, axis=1, keepdims=True), (128, 128))

    @peers(MEMBERS, sub)
    def _(p):
        copy(pack, packs.at[p], s_pack.at[p], r_pack.at[p], to_member(p)).wait_recv()

    hots = []
    for half in range(2):
        ident = jnp.zeros((1, 128), F32)
        for m in range(4 * half, 4 * half + 4):
            tile = packs[m, 2 * SLOTS:2 * SLOTS + 16, :].astype(F32)
            first = ((dp * MEMBERS + m) * n_pts + 1).astype(F32)
            ident = ident + 2.0 * tile[0:1, :] + tile[1:2, :] + first * tile[2:3, :]
        hots.append(jnp.where(target[...] + 1.0 == ident, 1.0, 0.0).astype(BF16))
    hot = jnp.concatenate(hots, axis=1)
    left = jnp.dot(hot, packs[:, 0:SLOTS, :].reshape(MEMBERS * SLOTS, 128), preferred_element_type=F32)
    right = jnp.dot(hot, packs[:, SLOTS:2 * SLOTS, :].reshape(MEMBERS * SLOTS, 128), preferred_element_type=F32)
    for q in range(Q):
        both = jnp.concatenate([left[per_q * q:per_q * (q + 1)], right[per_q * q:per_q * (q + 1)]], axis=0)
        dense[q] = both.astype(BF16)

    @far_first(Q, q_me)
    def _(p):
        copy(dense.at[p], drecv.at[q_me], s_d.at[p], r_d.at[q_me], to_plane(p)).start()

    @peers(CHIPS, chip)
    def _(p):
        copy(pts.at[sub], pts.at[sub], s_pts.at[p], r_pts.at[chip], to_chip(p)).start()

    copy(pts.at[sub], pts.at[sub], s_sib.at[chip], r_sib.at[chip], sibling).start()

    psum[...] = dense[q_me].astype(F32)

    @far_first(Q, q_me)
    def _(p):
        copy(dense.at[p], drecv.at[p], s_d.at[p], r_d.at[p], to_plane(p)).wait_recv()
        psum[...] += drecv[p].astype(F32)

    rsend[...] = psum[...].astype(BF16)

    @far_first(R, high)
    def _(p):
        copy(rsend, rrecv.at[high], s_r.at[p], r_r.at[high], to_ring(p)).start()

    @far_first(R, high)
    def _(p):
        copy(rsend, rrecv.at[p], s_r.at[p], r_r.at[p], to_ring(p)).wait_recv()
        psum[...] += rrecv[p].astype(F32)

    csend[...] = psum[...].astype(BF16)

    def wide_peers(b):
        def wrap(body):
            def step(i, carry):
                body(lax.rem(x + b, X) * 4 + lax.rem(low + i, 4))
                return carry
            lax.fori_loop(0 if b else 1, 4, step, 0)
        return wrap

    for b in (2, 3, 1, 0):
        @wide_peers(b)
        def _(p):
            copy(csend, c_buf.at[q_me], s_c.at[p], r_c.at[q_me], to_plane(p)).start()

    c_buf[q_me] = csend[...]

    @peers(CHIPS, chip)
    def _(p):
        slot = pts.at[p * CORES + core]
        copy(slot, slot, s_pts.at[p], r_pts.at[p], to_chip(p)).wait_recv()
        copy(slot, slot, s_sib.at[p], r_sib.at[p], sibling).start()

    nt = (((1,), (1,)), ((), ()))

    def norms(idx):
        wide = pts[idx].astype(F32)
        square = wide * wide
        top = square.astype(BF16)
        rest = (square - top.astype(F32)).astype(BF16)
        ones = jnp.ones((8, wide.shape[1]), BF16)
        pn = (lax.dot_general(ones, top, nt, preferred_element_type=F32)
              + lax.dot_general(ones, rest, nt, preferred_element_type=F32))
        pn_buf[idx] = pn[0:1, :]

    @peers(CHIPS + 1, 0)
    def _(i):
        norms(lax.rem(chip + i, CHIPS) * CORES + core)

    @peers(CHIPS + 1, 0)
    def _(i):
        p = lax.rem(chip + i, CHIPS)
        slot = pts.at[p * CORES + 1 - core]
        copy(slot, slot, s_sib.at[p], r_sib.at[p], sibling).wait_recv()
        norms(p * CORES + 1 - core)

    diag = iota((per_x, 128), 0) == iota((per_x, 128), 1)
    highest = []
    for pair in ((2, 1), (3, 0)):
        lefts, rights = [], []
        for b in pair:
            @wide_peers(b)
            def _(p):
                copy(csend, c_buf.at[p], s_c.at[p], r_c.at[p], to_plane(p)).wait_recv()

            for l in range(4):
                rows_q = c_buf[lax.rem(x + b, X) * 4 + l].astype(F32)
                lefts.append(rows_q[0:per_q])
                rights.append(rows_q[per_q:2 * per_q])
        chosen = jnp.concatenate([jnp.concatenate(lefts, axis=0), jnp.concatenate(rights, axis=0)], axis=1)
        cn = jnp.sum(chosen * chosen, axis=1, keepdims=True)
        twice = (2.0 * chosen).astype(BF16)
        weights, peaks, mass = [], [], None
        for m in range(MEMBERS):
            dots = lax.dot_general(twice, pts[m], nt, preferred_element_type=F32)
            less = dots - cn
            peaks.append(jnp.max(less, axis=0, keepdims=True))
            weight = jnp.exp2((less - pn_buf[m]) * SCALE).astype(BF16)
            weights.append(weight)
            wide_w = weight.astype(F32)
            for t in range(n_pts // 128):
                piece = wide_w[:, 128 * t:128 * (t + 1)]
                mass = piece if mass is None else mass + piece
        sums = jnp.dot(jnp.concatenate(weights, axis=1), pts[...].reshape(MEMBERS * n_pts, -1),
                       preferred_element_type=F32)
        highest.append(peaks)
        total = jnp.sum(mass, axis=1, keepdims=True)
        for k, b in enumerate(pair):
            dest = fsend.at[b]
            lo, hi = per_x * k, per_x * (k + 1)
            dest[0:per_x, :] = sums[lo:hi, 0:128]
            dest[per_x:2 * per_x, :] = sums[lo:hi, 128:256]
            line = jnp.sum(jnp.where(diag, total[lo:hi], 0.0), axis=0, keepdims=True)
            dest[2 * per_x:2 * per_x + 8, :] = jnp.broadcast_to(line, (8, 128))
            if b:
                p = lax.rem(x + b, X)
                copy(dest, frecv.at[x], s_f.at[p], r_f.at[x], to_x(p)).start()

    for m in range(MEMBERS):
        near = pn_buf[m] - jnp.maximum(highest[0][m], highest[1][m])
        for t in range(n_pts // 128):
            minsend[m, t:t + 1, :] = near[:, 128 * t:128 * (t + 1)]

    @peers(MEMBERS, sub)
    def _(p):
        copy(minsend.at[p], minrecv.at[sub], s_m.at[p], r_m.at[sub], to_member(p)).start()

    fsum[...] = fsend[0]

    @far_first(X, x)
    def _(p):
        copy(frecv.at[p], frecv.at[p], s_f.at[p], r_f.at[p], to_x(p)).wait_recv()
        fsum[...] += frecv[p]

    for k in range(Z):
        lo, hi = OUT_ROWS * k, OUT_ROWS * (k + 1)
        gsend[k, 0:OUT_ROWS, :] = fsum[lo:hi, :]
        gsend[k, OUT_ROWS:8, :] = fsum[2 * per_x:2 * per_x + 8 - OUT_ROWS, :]
        gsend[k, 8:8 + OUT_ROWS, :] = fsum[per_x + lo:per_x + hi, :]
        gsend[k, 8 + OUT_ROWS:16, :] = jnp.zeros((8 - OUT_ROWS, 128), F32)

    @far_first(Z, z)
    def _(p):
        copy(gsend.at[z_slot(p)], grecv.at[z], s_g.at[p], r_g.at[z], to_z(p)).start()

    out_min[...] = minsend[sub]

    @peers(MEMBERS, sub)
    def _(p):
        copy(minsend.at[p], minrecv.at[p], s_m.at[p], r_m.at[p], to_member(p)).wait_recv()
        out_min[...] = jnp.minimum(out_min[...], minrecv[p])

    final = fsum.at[0:16]
    final[...] = gsend[k_me]

    @peers(Z, z)
    def _(p):
        copy(gsend.at[p], grecv.at[p], s_g.at[p], r_g.at[p], to_z(p)).wait_recv()
        final[...] += grecv[p]

    both = final[...]
    line = both[OUT_ROWS:OUT_ROWS + 1, :]
    pick = iota((8, 128), 1) == iota((8, 128), 0) + OUT_ROWS * k_me
    column = jnp.sum(jnp.where(pick, line, 0.0), axis=1, keepdims=True)
    out_cent[:, 0:128] = both[0:OUT_ROWS, :] / column[0:OUT_ROWS]
    out_cent[:, 128:256] = both[8:8 + OUT_ROWS, :] / column[0:OUT_ROWS]
    eye = iota((8, 128), 1) == iota((8, 128), 0)
    out_mass[...] = jnp.sum(jnp.where(eye, column, 0.0), axis=0, keepdims=True)

    @peers(MEMBERS, sub)
    def _(p):
        copy(pack, packs.at[sub], s_pack.at[p], r_pack.at[p], to_member(p)).wait_send()

    @peers(MEMBERS, sub)
    def _(p):
        copy(minsend.at[p], minrecv.at[p], s_m.at[p], r_m.at[p], to_member(p)).wait_send()

    @peers(CHIPS, chip)
    def _(p):
        slot = pts.at[p * CORES + core]
        copy(slot, slot, s_pts.at[p], r_pts.at[p], sibling).wait_send()
        copy(slot, slot, s_sib.at[p], r_sib.at[p], sibling).wait_send()

    copy(pts.at[sub], pts.at[sub], s_sib.at[chip], r_sib.at[chip], sibling).wait_send()

    @peers(Q, q_me)
    def _(p):
        copy(dense.at[p], drecv.at[p], s_d.at[p], r_d.at[p], sibling).wait_send()

    @peers(Q, q_me)
    def _(p):
        copy(csend, c_buf.at[p], s_c.at[p], r_c.at[p], sibling).wait_send()

    @peers(R, high)
    def _(p):
        copy(rsend, rrecv.at[p], s_r.at[p], r_r.at[p], sibling).wait_send()

    @peers(X, x)
    def _(p):
        copy(frecv.at[p], frecv.at[p], s_f.at[p], r_f.at[p], sibling).wait_send()

    @peers(Z, z)
    def _(p):
        copy(gsend.at[p], grecv.at[p], s_g.at[p], r_g.at[p], sibling).wait_send()


def on_device(points, candidates, owner_slot):
    n_pts, dim = points.shape
    per_q, per_x = R * OUT_ROWS, Z * OUT_ROWS
    rows = Q * per_q
    owner = owner_slot.reshape(-1, 128)
    vmem = pltpu.VMEM
    dma = pltpu.SemaphoreType.DMA
    scratch = [
        vmem((MEMBERS, n_pts, dim), BF16),
        vmem(candidates.shape, jnp.int32),
        vmem(owner.shape, jnp.int32),
        vmem((2 * SLOTS + 16, 128), BF16),
        vmem((MEMBERS, 2 * SLOTS + 16, 128), BF16),
        vmem((rows, 128), F32),
        vmem((Q, 2 * per_q, 128), BF16),
        vmem((Q, 2 * per_q, 128), BF16),
        vmem((2 * per_q, 128), F32),
        vmem((2 * per_q, 128), BF16),
        vmem((R, 2 * per_q, 128), BF16),
        vmem((2 * per_q, 128), BF16),
        vmem((Q, 2 * per_q, 128), BF16),
        vmem((MEMBERS, 1, n_pts), F32),
        vmem((MEMBERS, n_pts // 128, 128), F32),
        vmem((MEMBERS, n_pts // 128, 128), F32),
        vmem((X, 2 * per_x + 8, 128), F32),
        vmem((X, 2 * per_x + 8, 128), F32),
        vmem((2 * per_x + 8, 128), F32),
        vmem((Z, 16, 128), F32),
        vmem((Z, 16, 128), F32),
        dma((3,)),
    ]
    for n in (MEMBERS, CHIPS, CHIPS, Q, R, Q, X, Z, MEMBERS):
        scratch += [dma((n,)), dma((n,))]
    cent, mass, near = pl.pallas_call(
        kernel,
        out_shape=(
            jax.ShapeDtypeStruct((OUT_ROWS, dim), F32),
            jax.ShapeDtypeStruct((1, 128), F32),
            jax.ShapeDtypeStruct((n_pts // 128, 128), F32),
        ),
        in_specs=[pl.BlockSpec(memory_space=pltpu.HBM)] * 3,
        out_specs=[pl.BlockSpec(memory_space=vmem)] * 3,
        scratch_shapes=scratch,
        compiler_params=pltpu.CompilerParams(
            collective_id=0, has_side_effects=True, vmem_limit_bytes=55213 * 2 ** 10),
    )(points, candidates, owner)
    return cent, mass[0, 0:OUT_ROWS], near.reshape(-1)


def solution(mesh):
    return jax.shard_map(
        on_device,
        mesh=mesh,
        in_specs=(P(("dp", "sub"), None), P(), P()),
        out_specs=(P(("dp", "sub"), None), P(("dp", "sub")), P(("dp", "sub"))),
        check_vma=False,
    )
```

```python
import math

import jax
import jax.numpy as jnp
from jax import lax
from jax.experimental import pallas as pl
from jax.experimental.pallas import tpu as pltpu
from jax.sharding import PartitionSpec as P

MESH = pl.DeviceIdType.MESH
F32 = jnp.float32
BF16 = jnp.bfloat16
CORES = 2
CHIPS = 4
MEMBERS = CHIPS * CORES
OUT_ROWS = 6
SLOTS = 32
SCALE = 4.0 * math.log2(math.e)


Q, R = 16, 4
X, Z = 4, 16
PACKED = 2 * OUT_ROWS + 1


def iota(shape, dim):
    return lax.broadcasted_iota(jnp.int32, shape, dim)


def kernel(pts_hbm, cand_hbm, owner_hbm, out_cent, out_mass, out_min,
           pts, cand, owner, pack, packs, target, dense, drecv, psum, rsend, rrecv, csend, c_buf,
           pn_buf, minsend, minrecv, fsend, frecv, fsum, gsend, grecv,
           s_in, s_pack, r_pack, s_pts, r_pts, s_sib, r_sib, s_d, r_d, s_r, r_r, s_c, r_c,
           s_f, r_f, s_g, r_g, s_m, r_m):
    per_q = R * OUT_ROWS
    per_x = Z * OUT_ROWS
    rows = Q * per_q
    n_pts = pts_hbm.shape[0]
    rounds, per_round = cand.shape
    tiles = per_round // 128
    dp, sub = lax.axis_index("dp"), lax.axis_index("sub")
    z, x, chip, core = dp // X, dp % X, sub // CORES, sub % CORES
    low, high = z % 4, z // 4
    q_me = x * 4 + low
    device = dp * MEMBERS + sub
    sibling = (dp, chip * CORES + 1 - core)

    def to_member(m):
        return dp, m

    def to_chip(p):
        return dp, p * CORES + core

    def to_plane(q):
        return (high * 4 + q % 4) * X + q // 4, sub

    def to_ring(r):
        return (r * 4 + low) * X + x, sub

    def to_x(p):
        return z * X + p, sub

    def to_z(p):
        return p * X + x, sub

    def copy(src, dst, send, recv, where):
        return pltpu.make_async_remote_copy(
            src_ref=src, dst_ref=dst, send_sem=send, recv_sem=recv, device_id=where, device_id_type=MESH)

    def peers(n, me):
        def wrap(body):
            def step(i, carry):
                body(lax.rem(me + i, n))
                return carry
            lax.fori_loop(1, n, step, 0)
        return wrap

    def far_first(n, me):
        def wrap(body):
            def step(i, carry):
                body(lax.rem(me + n // 2 + (1 - 2 * (i % 2)) * ((i + 1) // 2), n))
                return carry
            lax.fori_loop(0, n - 1, step, 0)
        return wrap

    barrier = pltpu.get_barrier_semaphore()
    for order, n, me, to in ((far_first, Z, z, to_z), (peers, Q, q_me, to_plane), (peers, MEMBERS, sub, to_member)):
        @order(n, me)
        def _(p, to=to):
            pl.semaphore_signal(barrier, inc=1, device_id=to(p), device_id_type=MESH)

    loads = [
        pltpu.make_async_copy(cand_hbm, cand, s_in.at[0]),
        pltpu.make_async_copy(pts_hbm, pts.at[sub], s_in.at[1]),
        pltpu.make_async_copy(owner_hbm, owner, s_in.at[2]),
    ]
    for load in loads:
        load.start()
    for load in loads:
        load.wait()

    step = 64
    hits = []
    for lo in range(0, n_pts, step):
        local = iota((step, 128), 0) + (device * n_pts + lo)
        hit = jnp.zeros((step, 128), F32)
        for rnd in range(rounds):
            for t in range(tiles):
                hit = jnp.where(local == cand[rnd:rnd + 1, 128 * t:128 * (t + 1)], 1.0, hit)
        hits.append(jnp.max(hit, axis=1, keepdims=True))
    hit = jnp.concatenate(hits, axis=0)
    below = jnp.where(iota((n_pts, n_pts), 1) < iota((n_pts, n_pts), 0), 1.0, 0.0).astype(BF16)
    rank = jnp.dot(below, jnp.broadcast_to(hit, (n_pts, 128)).astype(BF16), preferred_element_type=F32)
    rank = rank.astype(jnp.int32)
    lane = iota((n_pts, 128), 1)
    sel = jnp.where((rank == lane) & (lane < SLOTS), hit, 0.0).astype(BF16)
    picked = lax.dot_general(sel, pts[sub], (((0,), (0,)), ((), ())), preferred_element_type=F32)
    moved = jnp.where(rank + (sub % 4) * SLOTS == lane, hit, 0.0)
    rowno = iota((n_pts, 128), 0)
    upper = jnp.sum(moved * (rowno >> 1).astype(F32), axis=0, keepdims=True)
    lower = jnp.sum(moved * (rowno & 1).astype(F32), axis=0, keepdims=True)
    used = jnp.sum(moved, axis=0, keepdims=True)
    which = iota((16, 128), 0)
    ids = jnp.where(which == 0, upper, jnp.where(which == 1, lower, jnp.where(which == 2, used, 0.0)))
    pack[0:SLOTS, :] = picked[0:SLOTS, 0:128].astype(BF16)
    pack[SLOTS:2 * SLOTS, :] = picked[0:SLOTS, 128:256].astype(BF16)
    pack[2 * SLOTS:2 * SLOTS + 16, :] = ids.astype(BF16)
    packs[sub] = pack[...]

    pl.semaphore_wait(barrier, MEMBERS + Q + Z - 3)

    @peers(MEMBERS, sub)
    def _(p):
        copy(pack, packs.at[sub], s_pack.at[p], r_pack.at[sub], to_member(p)).start()

    for blk in range(rows // 128):
        i = iota((128, 128), 0) + 128 * blk
        group = (i * 10923) >> 16
        q, r, j = group >> 2, group & 3, i - group * OUT_ROWS
        slot = ((((r << 2) + (q & 3)) * X + (q >> 2)) * MEMBERS + sub) * OUT_ROWS + j
        found = jnp.zeros((128, 128), F32)
        for rnd in range(rounds):
            for t in range(tiles):
                c = cand[rnd:rnd + 1, 128 * t:128 * (t + 1)].astype(F32)
                o = owner[rnd * tiles + t:rnd * tiles + t + 1, :]
                found = jnp.where(slot == o, c, found)
        target[128 * blk:128 * (blk + 1), :] = jnp.broadcast_to(
            jnp.sum(found, axis=1, keepdims=True), (128, 128))

    @peers(MEMBERS, sub)
    def _(p):
        copy(pack, packs.at[p], s_pack.at[p], r_pack.at[p], to_member(p)).wait_recv()

    hots = []
    for half in range(2):
        ident = jnp.zeros((1, 128), F32)
        for m in range(4 * half, 4 * half + 4):
            tile = packs[m, 2 * SLOTS:2 * SLOTS + 16, :].astype(F32)
            first = ((dp * MEMBERS + m) * n_pts + 1).astype(F32)
            ident = ident + 2.0 * tile[0:1, :] + tile[1:2, :] + first * tile[2:3, :]
        hots.append(jnp.where(target[...] + 1.0 == ident, 1.0, 0.0).astype(BF16))
    hot = jnp.concatenate(hots, axis=1)
    left = jnp.dot(hot, packs[:, 0:SLOTS, :].reshape(MEMBERS * SLOTS, 128), preferred_element_type=F32)
    right = jnp.dot(hot, packs[:, SLOTS:2 * SLOTS, :].reshape(MEMBERS * SLOTS, 128), preferred_element_type=F32)
    for q in range(Q):
        both = jnp.concatenate([left[per_q * q:per_q * (q + 1)], right[per_q * q:per_q * (q + 1)]], axis=0)
        dense[q] = both.astype(BF16)

    @far_first(Q, q_me)
    def _(p):
        copy(dense.at[p], drecv.at[q_me], s_d.at[p], r_d.at[q_me], to_plane(p)).start()

    @peers(CHIPS, chip)
    def _(p):
        copy(pts.at[sub], pts.at[sub], s_pts.at[p], r_pts.at[chip], to_chip(p)).start()

    copy(pts.at[sub], pts.at[sub], s_sib.at[chip], r_sib.at[chip], sibling).start()

    psum[...] = dense[q_me].astype(F32)

    @far_first(Q, q_me)
    def _(p):
        copy(dense.at[p], drecv.at[p], s_d.at[p], r_d.at[p], to_plane(p)).wait_recv()
        psum[...] += drecv[p].astype(F32)

    rsend[...] = psum[...].astype(BF16)

    @far_first(R, high)
    def _(p):
        copy(rsend, rrecv.at[high], s_r.at[p], r_r.at[high], to_ring(p)).start()

    @far_first(R, high)
    def _(p):
        copy(rsend, rrecv.at[p], s_r.at[p], r_r.at[p], to_ring(p)).wait_recv()
        psum[...] += rrecv[p].astype(F32)

    csend[...] = psum[...].astype(BF16)

    def wide_peers(b):
        def wrap(body):
            def step(i, carry):
                body(lax.rem(x + b, X) * 4 + lax.rem(low + i, 4))
                return carry
            lax.fori_loop(0 if b else 1, 4, step, 0)
        return wrap

    for b in (2, 3, 1, 0):
        @wide_peers(b)
        def _(p):
            copy(csend, c_buf.at[q_me], s_c.at[p], r_c.at[q_me], to_plane(p)).start()

    c_buf[q_me] = csend[...]

    @peers(CHIPS, chip)
    def _(p):
        slot = pts.at[p * CORES + core]
        copy(slot, slot, s_pts.at[p], r_pts.at[p], to_chip(p)).wait_recv()
        copy(slot, slot, s_sib.at[p], r_sib.at[p], sibling).start()

    nt = (((1,), (1,)), ((), ()))

    def norms(idx):
        wide = pts[idx].astype(F32)
        square = wide * wide
        top = square.astype(BF16)
        rest = (square - top.astype(F32)).astype(BF16)
        ones = jnp.ones((8, wide.shape[1]), BF16)
        pn = (lax.dot_general(ones, top, nt, preferred_element_type=F32)
              + lax.dot_general(ones, rest, nt, preferred_element_type=F32))
        pn_buf[idx] = pn[0:1, :]

    @peers(CHIPS + 1, 0)
    def _(i):
        norms(lax.rem(chip + i, CHIPS) * CORES + core)

    @peers(CHIPS + 1, 0)
    def _(i):
        p = lax.rem(chip + i, CHIPS)
        slot = pts.at[p * CORES + 1 - core]
        copy(slot, slot, s_sib.at[p], r_sib.at[p], sibling).wait_recv()
        norms(p * CORES + 1 - core)

    diag = iota((per_q, 128), 0) == iota((per_q, 128), 1)
    highest = []
    for pair in ((2, 1), (3, 0)):
        lefts, rights = [], []
        for b in pair:
            @wide_peers(b)
            def _(p):
                copy(csend, c_buf.at[p], s_c.at[p], r_c.at[p], to_plane(p)).wait_recv()

            for l in range(4):
                rows_q = c_buf[lax.rem(x + b, X) * 4 + l].astype(F32)
                lefts.append(rows_q[0:per_q])
                rights.append(rows_q[per_q:2 * per_q])
        chosen = jnp.concatenate([jnp.concatenate(lefts, axis=0), jnp.concatenate(rights, axis=0)], axis=1)
        cn = jnp.sum(chosen * chosen, axis=1, keepdims=True)
        twice = (2.0 * chosen).astype(BF16)
        weights, peaks, mass = [], [], None
        for m in range(MEMBERS):
            dots = lax.dot_general(twice, pts[m], nt, preferred_element_type=F32)
            less = dots - cn
            peaks.append(jnp.max(less, axis=0, keepdims=True))
            weight = jnp.exp2((less - pn_buf[m]) * SCALE).astype(BF16)
            weights.append(weight)
            wide_w = weight.astype(F32)
            for t in range(n_pts // 128):
                piece = wide_w[:, 128 * t:128 * (t + 1)]
                mass = piece if mass is None else mass + piece
        sums = jnp.dot(jnp.concatenate(weights, axis=1), pts[...].reshape(MEMBERS * n_pts, -1),
                       preferred_element_type=F32)
        highest.append(peaks)
        total = jnp.sum(mass, axis=1, keepdims=True)
        for l in range(4):
            for k, b in enumerate(pair):
                dest = fsend.at[b, l]
                lo = per_x * k + per_q * l
                dest[0:per_q, :] = sums[lo:lo + per_q, 0:128]
                dest[per_q:2 * per_q, :] = sums[lo:lo + per_q, 128:256]
                line = jnp.sum(jnp.where(diag, total[lo:lo + per_q], 0.0), axis=0, keepdims=True)
                dest[2 * per_q:2 * per_q + 8, :] = jnp.broadcast_to(line, (8, 128))
                if b:
                    p = lax.rem(x + b, X)
                    copy(dest, frecv.at[x, l], s_f.at[p, l], r_f.at[x, l], to_x(p)).start()

    for l in range(4):
        part = fsend[0, l]
        for b in (1, 2, 3):
            p = lax.rem(x + b, X)
            piece = frecv.at[p, l]
            copy(piece, piece, s_f.at[p, l], r_f.at[p, l], sibling).wait_recv()
            part = part + piece[...]
        fsum[l] = part
        for r in range(R):
            p = r * 4 + l
            lo = OUT_ROWS * r
            gsend[p, 0:OUT_ROWS, :] = fsum[l, lo:lo + OUT_ROWS, :]
            gsend[p, OUT_ROWS:OUT_ROWS + 1, :] = fsum[l, 2 * per_q:2 * per_q + 1, :]
            gsend[p, OUT_ROWS + 1:PACKED, :] = fsum[l, per_q + lo:per_q + lo + OUT_ROWS, :]

            @pl.when(p != z)
            def _():
                copy(gsend.at[p, 0:PACKED], grecv.at[z, 0:PACKED], s_g.at[p], r_g.at[z], to_z(p)).start()

    for m in range(MEMBERS):
        near = pn_buf[m] - jnp.maximum(highest[0][m], highest[1][m])
        for t in range(n_pts // 128):
            minsend[m, t:t + 1, :] = near[:, 128 * t:128 * (t + 1)]

    @peers(MEMBERS, sub)
    def _(p):
        copy(minsend.at[p], minrecv.at[sub], s_m.at[p], r_m.at[sub], to_member(p)).start()

    @peers(MEMBERS, sub)
    def _(p):
        copy(pack, packs.at[sub], s_pack.at[p], r_pack.at[p], to_member(p)).wait_send()

    @peers(CHIPS, chip)
    def _(p):
        slot = pts.at[p * CORES + core]
        copy(slot, slot, s_pts.at[p], r_pts.at[p], sibling).wait_send()
        copy(slot, slot, s_sib.at[p], r_sib.at[p], sibling).wait_send()

    copy(pts.at[sub], pts.at[sub], s_sib.at[chip], r_sib.at[chip], sibling).wait_send()

    @peers(Q, q_me)
    def _(p):
        copy(dense.at[p], drecv.at[p], s_d.at[p], r_d.at[p], sibling).wait_send()

    @peers(Q, q_me)
    def _(p):
        copy(csend, c_buf.at[p], s_c.at[p], r_c.at[p], sibling).wait_send()

    @peers(R, high)
    def _(p):
        copy(rsend, rrecv.at[p], s_r.at[p], r_r.at[p], sibling).wait_send()

    @peers(X, x)
    def _(p):
        for l in range(4):
            piece = frecv.at[p, l]
            copy(piece, piece, s_f.at[p, l], r_f.at[p, l], sibling).wait_send()

    out_min[...] = minsend[sub]

    @peers(MEMBERS, sub)
    def _(p):
        copy(minsend.at[p], minrecv.at[p], s_m.at[p], r_m.at[p], to_member(p)).wait_recv()
        out_min[...] = jnp.minimum(out_min[...], minrecv[p])

    @peers(MEMBERS, sub)
    def _(p):
        copy(minsend.at[p], minrecv.at[p], s_m.at[p], r_m.at[p], to_member(p)).wait_send()

    final = fsum.at[0, 0:16]
    final[0:PACKED, :] = gsend[z, 0:PACKED, :]

    @peers(Z, z)
    def _(p):
        piece = grecv.at[p, 0:PACKED]
        copy(piece, piece, s_g.at[p], r_g.at[p], to_z(p)).wait_send()

    @peers(Z, z)
    def _(p):
        piece = grecv.at[p, 0:PACKED]
        copy(piece, piece, s_g.at[p], r_g.at[p], to_z(p)).wait_recv()
        final[0:PACKED, :] += piece[...]

    both = final[...]
    line = both[OUT_ROWS:OUT_ROWS + 1, :]
    pick = iota((8, 128), 1) == iota((8, 128), 0) + OUT_ROWS * high
    column = jnp.sum(jnp.where(pick, line, 0.0), axis=1, keepdims=True)
    out_cent[:, 0:128] = both[0:OUT_ROWS, :] / column[0:OUT_ROWS]
    out_cent[:, 128:256] = both[OUT_ROWS + 1:PACKED, :] / column[0:OUT_ROWS]
    eye = iota((8, 128), 1) == iota((8, 128), 0)
    out_mass[...] = jnp.sum(jnp.where(eye, column, 0.0), axis=0, keepdims=True)


def on_device(points, candidates, owner_slot):
    n_pts, dim = points.shape
    per_q, per_x = R * OUT_ROWS, Z * OUT_ROWS
    rows = Q * per_q
    owner = owner_slot.reshape(-1, 128)
    vmem = pltpu.VMEM
    dma = pltpu.SemaphoreType.DMA
    scratch = [
        vmem((MEMBERS, n_pts, dim), BF16),
        vmem(candidates.shape, jnp.int32),
        vmem(owner.shape, jnp.int32),
        vmem((2 * SLOTS + 16, 128), BF16),
        vmem((MEMBERS, 2 * SLOTS + 16, 128), BF16),
        vmem((rows, 128), F32),
        vmem((Q, 2 * per_q, 128), BF16),
        vmem((Q, 2 * per_q, 128), BF16),
        vmem((2 * per_q, 128), F32),
        vmem((2 * per_q, 128), BF16),
        vmem((R, 2 * per_q, 128), BF16),
        vmem((2 * per_q, 128), BF16),
        vmem((Q, 2 * per_q, 128), BF16),
        vmem((MEMBERS, 1, n_pts), F32),
        vmem((MEMBERS, n_pts // 128, 128), F32),
        vmem((MEMBERS, n_pts // 128, 128), F32),
        vmem((X, 4, 2 * per_q + 8, 128), F32),
        vmem((X, 4, 2 * per_q + 8, 128), F32),
        vmem((4, 2 * per_q + 8, 128), F32),
        vmem((Z, 16, 128), F32),
        vmem((Z, 16, 128), F32),
        dma((3,)),
    ]
    for n in ((MEMBERS,), (CHIPS,), (CHIPS,), (Q,), (R,), (Q,), (X, 4), (Z,), (MEMBERS,)):
        scratch += [dma(n), dma(n)]
    cent, mass, near = pl.pallas_call(
        kernel,
        out_shape=(
            jax.ShapeDtypeStruct((OUT_ROWS, dim), F32),
            jax.ShapeDtypeStruct((1, 128), F32),
            jax.ShapeDtypeStruct((n_pts // 128, 128), F32),
        ),
        in_specs=[pl.BlockSpec(memory_space=pltpu.HBM)] * 3,
        out_specs=[pl.BlockSpec(memory_space=vmem)] * 3,
        scratch_shapes=scratch,
        compiler_params=pltpu.CompilerParams(
            collective_id=0, has_side_effects=True, vmem_limit_bytes=55213 * 2 ** 10),
    )(points, candidates, owner)
    return cent, mass[0, 0:OUT_ROWS], near.reshape(-1)


def solution(mesh):
    return jax.shard_map(
        on_device,
        mesh=mesh,
        in_specs=(P(("dp", "sub"), None), P(), P()),
        out_specs=(P(("dp", "sub"), None), P(("dp", "sub")), P(("dp", "sub"))),
        check_vma=False,
    )
```

```python
import math

import jax
import jax.numpy as jnp
from jax import lax
from jax.experimental import pallas as pl
from jax.experimental.pallas import tpu as pltpu
from jax.sharding import PartitionSpec as P

MESH = pl.DeviceIdType.MESH
F32 = jnp.float32
BF16 = jnp.bfloat16
CORES = 2
CHIPS = 4
MEMBERS = CHIPS * CORES
OUT_ROWS = 6
SLOTS = 32
SCALE = 4.0 * math.log2(math.e)


Q, R = 16, 4
X, Z = 4, 16
PACKED = 2 * OUT_ROWS + 1


def iota(shape, dim):
    return lax.broadcasted_iota(jnp.int32, shape, dim)


def kernel(pts_hbm, cand_hbm, owner_hbm, out_sums, out_min,
           pts, cand, owner, pack, packs, target, dense, drecv, psum, rsend, rrecv, csend, c_buf,
           pn_buf, minsend, minrecv, fsend, frecv, fsum, gsend, grecv,
           s_in, s_pack, r_pack, s_pts, r_pts, s_sib, r_sib, s_d, r_d, s_r, r_r, s_c, r_c,
           s_f, r_f, s_g, r_g, s_m, r_m):
    per_q = R * OUT_ROWS
    per_x = Z * OUT_ROWS
    rows = Q * per_q
    n_pts = pts_hbm.shape[0]
    rounds, per_round = cand.shape
    tiles = per_round // 128
    dp, sub = lax.axis_index("dp"), lax.axis_index("sub")
    z, x, chip, core = dp // X, dp % X, sub // CORES, sub % CORES
    low, high = z % 4, z // 4
    q_me = x * 4 + low
    device = dp * MEMBERS + sub
    sibling = (dp, chip * CORES + 1 - core)

    def to_member(m):
        return dp, m

    def to_chip(p):
        return dp, p * CORES + core

    def to_plane(q):
        return (high * 4 + q % 4) * X + q // 4, sub

    def to_ring(r):
        return (r * 4 + low) * X + x, sub

    def to_x(p):
        return z * X + p, sub

    def to_z(p):
        return p * X + x, sub

    def copy(src, dst, send, recv, where):
        return pltpu.make_async_remote_copy(
            src_ref=src, dst_ref=dst, send_sem=send, recv_sem=recv, device_id=where, device_id_type=MESH)

    def peers(n, me):
        def wrap(body):
            def step(i, carry):
                body(lax.rem(me + i, n))
                return carry
            lax.fori_loop(1, n, step, 0)
        return wrap

    def far_first(n, me):
        def wrap(body):
            def step(i, carry):
                body(lax.rem(me + n // 2 + (1 - 2 * (i % 2)) * ((i + 1) // 2), n))
                return carry
            lax.fori_loop(0, n - 1, step, 0)
        return wrap

    barrier = pltpu.get_barrier_semaphore()
    for order, n, me, to in ((far_first, Z, z, to_z), (peers, Q, q_me, to_plane), (peers, MEMBERS, sub, to_member)):
        @order(n, me)
        def _(p, to=to):
            pl.semaphore_signal(barrier, inc=1, device_id=to(p), device_id_type=MESH)

    loads = [
        pltpu.make_async_copy(cand_hbm, cand, s_in.at[0]),
        pltpu.make_async_copy(pts_hbm, pts.at[sub], s_in.at[1]),
        pltpu.make_async_copy(owner_hbm, owner, s_in.at[2]),
    ]
    for load in loads:
        load.start()
    for load in loads:
        load.wait()

    step = 64
    hits = []
    for lo in range(0, n_pts, step):
        local = iota((step, 128), 0) + (device * n_pts + lo)
        hit = jnp.zeros((step, 128), F32)
        for rnd in range(rounds):
            for t in range(tiles):
                hit = jnp.where(local == cand[rnd:rnd + 1, 128 * t:128 * (t + 1)], 1.0, hit)
        hits.append(jnp.max(hit, axis=1, keepdims=True))
    hit = jnp.concatenate(hits, axis=0)
    below = jnp.where(iota((n_pts, n_pts), 1) < iota((n_pts, n_pts), 0), 1.0, 0.0).astype(BF16)
    rank = jnp.dot(below, jnp.broadcast_to(hit, (n_pts, 128)).astype(BF16), preferred_element_type=F32)
    rank = rank.astype(jnp.int32)
    lane = iota((n_pts, 128), 1)
    sel = jnp.where((rank == lane) & (lane < SLOTS), hit, 0.0).astype(BF16)
    picked = lax.dot_general(sel, pts[sub], (((0,), (0,)), ((), ())), preferred_element_type=F32)
    moved = jnp.where(rank + (sub % 4) * SLOTS == lane, hit, 0.0)
    rowno = iota((n_pts, 128), 0)
    upper = jnp.sum(moved * (rowno >> 1).astype(F32), axis=0, keepdims=True)
    lower = jnp.sum(moved * (rowno & 1).astype(F32), axis=0, keepdims=True)
    used = jnp.sum(moved, axis=0, keepdims=True)
    which = iota((16, 128), 0)
    ids = jnp.where(which == 0, upper, jnp.where(which == 1, lower, jnp.where(which == 2, used, 0.0)))
    pack[0:SLOTS, :] = picked[0:SLOTS, 0:128].astype(BF16)
    pack[SLOTS:2 * SLOTS, :] = picked[0:SLOTS, 128:256].astype(BF16)
    pack[2 * SLOTS:2 * SLOTS + 16, :] = ids.astype(BF16)
    packs[sub] = pack[...]

    pl.semaphore_wait(barrier, MEMBERS + Q + Z - 3)

    @peers(MEMBERS, sub)
    def _(p):
        copy(pack, packs.at[sub], s_pack.at[p], r_pack.at[sub], to_member(p)).start()

    for blk in range(rows // 128):
        i = iota((128, 128), 0) + 128 * blk
        group = (i * 10923) >> 16
        q, r, j = group >> 2, group & 3, i - group * OUT_ROWS
        slot = ((((r << 2) + (q & 3)) * X + (q >> 2)) * MEMBERS + sub) * OUT_ROWS + j
        found = jnp.zeros((128, 128), F32)
        for rnd in range(rounds):
            for t in range(tiles):
                c = cand[rnd:rnd + 1, 128 * t:128 * (t + 1)].astype(F32)
                o = owner[rnd * tiles + t:rnd * tiles + t + 1, :]
                found = jnp.where(slot == o, c, found)
        target[128 * blk:128 * (blk + 1), :] = jnp.broadcast_to(
            jnp.sum(found, axis=1, keepdims=True), (128, 128))

    @peers(MEMBERS, sub)
    def _(p):
        copy(pack, packs.at[p], s_pack.at[p], r_pack.at[p], to_member(p)).wait_recv()

    hots = []
    for half in range(2):
        ident = jnp.zeros((1, 128), F32)
        for m in range(4 * half, 4 * half + 4):
            tile = packs[m, 2 * SLOTS:2 * SLOTS + 16, :].astype(F32)
            first = ((dp * MEMBERS + m) * n_pts + 1).astype(F32)
            ident = ident + 2.0 * tile[0:1, :] + tile[1:2, :] + first * tile[2:3, :]
        hots.append(jnp.where(target[...] + 1.0 == ident, 1.0, 0.0).astype(BF16))
    hot = jnp.concatenate(hots, axis=1)
    left = jnp.dot(hot, packs[:, 0:SLOTS, :].reshape(MEMBERS * SLOTS, 128), preferred_element_type=F32)
    right = jnp.dot(hot, packs[:, SLOTS:2 * SLOTS, :].reshape(MEMBERS * SLOTS, 128), preferred_element_type=F32)
    for q in range(Q):
        both = jnp.concatenate([left[per_q * q:per_q * (q + 1)], right[per_q * q:per_q * (q + 1)]], axis=0)
        dense[q] = both.astype(BF16)

    @far_first(Q, q_me)
    def _(p):
        copy(dense.at[p], drecv.at[q_me], s_d.at[p], r_d.at[q_me], to_plane(p)).start()

    @peers(CHIPS, chip)
    def _(p):
        copy(pts.at[sub], pts.at[sub], s_pts.at[p], r_pts.at[chip], to_chip(p)).start()

    copy(pts.at[sub], pts.at[sub], s_sib.at[chip], r_sib.at[chip], sibling).start()

    psum[...] = dense[q_me].astype(F32)

    @far_first(Q, q_me)
    def _(p):
        copy(dense.at[p], drecv.at[p], s_d.at[p], r_d.at[p], to_plane(p)).wait_recv()
        psum[...] += drecv[p].astype(F32)

    rsend[...] = psum[...].astype(BF16)

    @far_first(R, high)
    def _(p):
        copy(rsend, rrecv.at[high], s_r.at[p], r_r.at[high], to_ring(p)).start()

    @far_first(R, high)
    def _(p):
        copy(rsend, rrecv.at[p], s_r.at[p], r_r.at[p], to_ring(p)).wait_recv()
        psum[...] += rrecv[p].astype(F32)

    csend[...] = psum[...].astype(BF16)

    def wide_peers(b):
        def wrap(body):
            def step(i, carry):
                body(lax.rem(x + b, X) * 4 + lax.rem(low + i, 4))
                return carry
            lax.fori_loop(0 if b else 1, 4, step, 0)
        return wrap

    for b in (2, 3, 1, 0):
        @wide_peers(b)
        def _(p):
            copy(csend, c_buf.at[q_me], s_c.at[p], r_c.at[q_me], to_plane(p)).start()

    c_buf[q_me] = csend[...]

    @peers(CHIPS, chip)
    def _(p):
        slot = pts.at[p * CORES + core]
        copy(slot, slot, s_pts.at[p], r_pts.at[p], to_chip(p)).wait_recv()
        copy(slot, slot, s_sib.at[p], r_sib.at[p], sibling).start()

    nt = (((1,), (1,)), ((), ()))

    def norms(idx):
        wide = pts[idx].astype(F32)
        square = wide * wide
        top = square.astype(BF16)
        rest = (square - top.astype(F32)).astype(BF16)
        ones = jnp.ones((8, wide.shape[1]), BF16)
        pn = (lax.dot_general(ones, top, nt, preferred_element_type=F32)
              + lax.dot_general(ones, rest, nt, preferred_element_type=F32))
        pn_buf[idx] = pn[0:1, :]

    @peers(CHIPS + 1, 0)
    def _(i):
        norms(lax.rem(chip + i, CHIPS) * CORES + core)

    @peers(CHIPS + 1, 0)
    def _(i):
        p = lax.rem(chip + i, CHIPS)
        slot = pts.at[p * CORES + 1 - core]
        copy(slot, slot, s_sib.at[p], r_sib.at[p], sibling).wait_recv()
        norms(p * CORES + 1 - core)

    diag = iota((per_q, 128), 0) == iota((per_q, 128), 1)
    highest = []
    for pair in ((2, 1), (3, 0)):
        lefts, rights = [], []
        for b in pair:
            @wide_peers(b)
            def _(p):
                copy(csend, c_buf.at[p], s_c.at[p], r_c.at[p], to_plane(p)).wait_recv()

            for l in range(4):
                rows_q = c_buf[lax.rem(x + b, X) * 4 + l].astype(F32)
                lefts.append(rows_q[0:per_q])
                rights.append(rows_q[per_q:2 * per_q])
        chosen = jnp.concatenate([jnp.concatenate(lefts, axis=0), jnp.concatenate(rights, axis=0)], axis=1)
        cn = jnp.sum(chosen * chosen, axis=1, keepdims=True)
        twice = (2.0 * chosen).astype(BF16)
        weights, peaks, mass = [], [], None
        for m in range(MEMBERS):
            dots = lax.dot_general(twice, pts[m], nt, preferred_element_type=F32)
            less = dots - cn
            peaks.append(jnp.max(less, axis=0, keepdims=True))
            weight = jnp.exp2((less - pn_buf[m]) * SCALE).astype(BF16)
            weights.append(weight)
            wide_w = weight.astype(F32)
            for t in range(n_pts // 128):
                piece = wide_w[:, 128 * t:128 * (t + 1)]
                mass = piece if mass is None else mass + piece
        sums = jnp.dot(jnp.concatenate(weights, axis=1), pts[...].reshape(MEMBERS * n_pts, -1),
                       preferred_element_type=F32)
        highest.append(peaks)
        total = jnp.sum(mass, axis=1, keepdims=True)
        for l in range(4):
            for k, b in enumerate(pair):
                dest = fsend.at[b, l]
                lo = per_x * k + per_q * l
                dest[0:per_q, :] = sums[lo:lo + per_q, 0:128]
                dest[per_q:2 * per_q, :] = sums[lo:lo + per_q, 128:256]
                line = jnp.sum(jnp.where(diag, total[lo:lo + per_q], 0.0), axis=0, keepdims=True)
                dest[2 * per_q:2 * per_q + 8, :] = jnp.broadcast_to(line, (8, 128))
                if b:
                    p = lax.rem(x + b, X)
                    copy(dest, frecv.at[x, l], s_f.at[p, l], r_f.at[x, l], to_x(p)).start()

    for l in range(4):
        part = fsend[0, l]
        for b in (1, 2, 3):
            p = lax.rem(x + b, X)
            piece = frecv.at[p, l]
            copy(piece, piece, s_f.at[p, l], r_f.at[p, l], sibling).wait_recv()
            part = part + piece[...]
        fsum[l] = part
        for r in range(R):
            p = r * 4 + l
            lo = OUT_ROWS * r
            gsend[p, 0:OUT_ROWS, :] = fsum[l, lo:lo + OUT_ROWS, :]
            gsend[p, OUT_ROWS:OUT_ROWS + 1, :] = fsum[l, 2 * per_q:2 * per_q + 1, :]
            gsend[p, OUT_ROWS + 1:PACKED, :] = fsum[l, per_q + lo:per_q + lo + OUT_ROWS, :]

            @pl.when(p != z)
            def _():
                copy(gsend.at[p, 0:PACKED], grecv.at[z, 0:PACKED], s_g.at[p], r_g.at[z], to_z(p)).start()

    for m in range(MEMBERS):
        near = pn_buf[m] - jnp.maximum(highest[0][m], highest[1][m])
        for t in range(n_pts // 128):
            minsend[m, t:t + 1, :] = near[:, 128 * t:128 * (t + 1)]

    @peers(MEMBERS, sub)
    def _(p):
        copy(minsend.at[p], minrecv.at[sub], s_m.at[p], r_m.at[sub], to_member(p)).start()

    @peers(MEMBERS, sub)
    def _(p):
        copy(pack, packs.at[sub], s_pack.at[p], r_pack.at[p], to_member(p)).wait_send()

    @peers(CHIPS, chip)
    def _(p):
        slot = pts.at[p * CORES + core]
        copy(slot, slot, s_pts.at[p], r_pts.at[p], sibling).wait_send()
        copy(slot, slot, s_sib.at[p], r_sib.at[p], sibling).wait_send()

    copy(pts.at[sub], pts.at[sub], s_sib.at[chip], r_sib.at[chip], sibling).wait_send()

    @peers(Q, q_me)
    def _(p):
        copy(dense.at[p], drecv.at[p], s_d.at[p], r_d.at[p], sibling).wait_send()

    @peers(Q, q_me)
    def _(p):
        copy(csend, c_buf.at[p], s_c.at[p], r_c.at[p], sibling).wait_send()

    @peers(R, high)
    def _(p):
        copy(rsend, rrecv.at[p], s_r.at[p], r_r.at[p], sibling).wait_send()

    @peers(X, x)
    def _(p):
        for l in range(4):
            piece = frecv.at[p, l]
            copy(piece, piece, s_f.at[p, l], r_f.at[p, l], sibling).wait_send()

    out_min[...] = minsend[sub]

    @peers(MEMBERS, sub)
    def _(p):
        copy(minsend.at[p], minrecv.at[p], s_m.at[p], r_m.at[p], to_member(p)).wait_recv()
        out_min[...] = jnp.minimum(out_min[...], minrecv[p])

    @peers(MEMBERS, sub)
    def _(p):
        copy(minsend.at[p], minrecv.at[p], s_m.at[p], r_m.at[p], to_member(p)).wait_send()

    final = fsum.at[0, 0:16]
    final[0:PACKED, :] = gsend[z, 0:PACKED, :]

    @peers(Z, z)
    def _(p):
        piece = grecv.at[p, 0:PACKED]
        copy(piece, piece, s_g.at[p], r_g.at[p], to_z(p)).wait_send()

    @peers(Z, z)
    def _(p):
        piece = grecv.at[p, 0:PACKED]
        copy(piece, piece, s_g.at[p], r_g.at[p], to_z(p)).wait_recv()
        final[0:PACKED, :] += piece[...]

    out_sums[...] = final[...]


def finish(sums, near, out_cent, out_mass, out_min):
    high = lax.axis_index("dp") // X // 4
    line = sums[OUT_ROWS:OUT_ROWS + 1, :]
    pick = iota((8, 128), 1) == iota((8, 128), 0) + OUT_ROWS * high
    column = jnp.sum(jnp.where(pick, line, 0.0), axis=1, keepdims=True)
    out_cent[:, 0:128] = sums[0:OUT_ROWS, :] / column[0:OUT_ROWS]
    out_cent[:, 128:256] = sums[OUT_ROWS + 1:PACKED, :] / column[0:OUT_ROWS]
    eye = iota((8, 128), 1) == iota((8, 128), 0)
    out_mass[...] = jnp.sum(jnp.where(eye, column, 0.0), axis=0, keepdims=True)[:, 0:OUT_ROWS]
    out_min[...] = near[...]


def on_device(points, candidates, owner_slot):
    n_pts, dim = points.shape
    per_q, per_x = R * OUT_ROWS, Z * OUT_ROWS
    rows = Q * per_q
    owner = owner_slot.reshape(-1, 128)
    vmem = pltpu.VMEM
    dma = pltpu.SemaphoreType.DMA
    scratch = [
        vmem((MEMBERS, n_pts, dim), BF16),
        vmem(candidates.shape, jnp.int32),
        vmem(owner.shape, jnp.int32),
        vmem((2 * SLOTS + 16, 128), BF16),
        vmem((MEMBERS, 2 * SLOTS + 16, 128), BF16),
        vmem((rows, 128), F32),
        vmem((Q, 2 * per_q, 128), BF16),
        vmem((Q, 2 * per_q, 128), BF16),
        vmem((2 * per_q, 128), F32),
        vmem((2 * per_q, 128), BF16),
        vmem((R, 2 * per_q, 128), BF16),
        vmem((2 * per_q, 128), BF16),
        vmem((Q, 2 * per_q, 128), BF16),
        vmem((MEMBERS, 1, n_pts), F32),
        vmem((MEMBERS, n_pts // 128, 128), F32),
        vmem((MEMBERS, n_pts // 128, 128), F32),
        vmem((X, 4, 2 * per_q + 8, 128), F32),
        vmem((X, 4, 2 * per_q + 8, 128), F32),
        vmem((4, 2 * per_q + 8, 128), F32),
        vmem((Z, 16, 128), F32),
        vmem((Z, 16, 128), F32),
        dma((3,)),
    ]
    for n in ((MEMBERS,), (CHIPS,), (CHIPS,), (Q,), (R,), (Q,), (X, 4), (Z,), (MEMBERS,)):
        scratch += [dma(n), dma(n)]
    sums, near = pl.pallas_call(
        kernel,
        out_shape=(
            jax.ShapeDtypeStruct((16, 128), F32),
            jax.ShapeDtypeStruct((n_pts // 128, 128), F32),
        ),
        in_specs=[pl.BlockSpec(memory_space=pltpu.HBM)] * 3,
        out_specs=[pl.BlockSpec(memory_space=vmem)] * 2,
        scratch_shapes=scratch,
        compiler_params=pltpu.CompilerParams(
            collective_id=0, has_side_effects=True, vmem_limit_bytes=55213 * 2 ** 10),
    )(points, candidates, owner)
    cent, mass, near = pl.pallas_call(
        finish,
        out_shape=(
            jax.ShapeDtypeStruct((OUT_ROWS, dim), F32),
            jax.ShapeDtypeStruct((1, OUT_ROWS), F32),
            jax.ShapeDtypeStruct((n_pts // 128, 128), F32),
        ),
        in_specs=[pl.BlockSpec(memory_space=vmem)] * 2,
        out_specs=[pl.BlockSpec(memory_space=vmem)] * 3,
        compiler_params=pltpu.CompilerParams(vmem_limit_bytes=2 ** 20),
    )(sums, near)
    return cent, mass.reshape(-1), near.reshape(-1)


def solution(mesh):
    return jax.shard_map(
        on_device,
        mesh=mesh,
        in_specs=(P(("dp", "sub"), None), P(), P()),
        out_specs=(P(("dp", "sub"), None), P(("dp", "sub")), P(("dp", "sub"))),
        check_vma=False,
    )
```

```python
import math

import jax
import jax.numpy as jnp
from jax import lax
from jax.experimental import pallas as pl
from jax.experimental.pallas import tpu as pltpu
from jax.sharding import PartitionSpec as P

MESH = pl.DeviceIdType.MESH
F32 = jnp.float32
BF16 = jnp.bfloat16
CORES = 2
CHIPS = 4
MEMBERS = CHIPS * CORES
OUT_ROWS = 6
SLOTS = 32
SCALE = 4.0 * math.log2(math.e)


Q, R = 16, 4
X, Z = 4, 16
PIECE = 2 * R * OUT_ROWS + 1
PACKED = 2 * OUT_ROWS + 1


def iota(shape, dim):
    return lax.broadcasted_iota(jnp.int32, shape, dim)


def kernel(pts_hbm, cand_hbm, owner_hbm, out_sums, out_min,
           pts, cand, owner, pack, packs, target, dense, drecv, psum, rsend, rrecv, csend, c_buf,
           pn_buf, minsend, minrecv, fsend, frecv, fsum, gsend, grecv,
           s_in, s_pack, r_pack, s_pts, r_pts, s_sib, r_sib, s_d, r_d, s_r, r_r, s_c, r_c,
           s_f, r_f, s_g, r_g, s_m, r_m):
    per_q = R * OUT_ROWS
    per_x = Z * OUT_ROWS
    rows = Q * per_q
    n_pts = pts_hbm.shape[0]
    rounds, per_round = cand.shape
    tiles = per_round // 128
    dp, sub = lax.axis_index("dp"), lax.axis_index("sub")
    z, x, chip, core = dp // X, dp % X, sub // CORES, sub % CORES
    low, high = z % 4, z // 4
    q_me = x * 4 + low
    device = dp * MEMBERS + sub
    sibling = (dp, chip * CORES + 1 - core)

    def to_member(m):
        return dp, m

    def to_chip(p):
        return dp, p * CORES + core

    def to_plane(q):
        return (high * 4 + q % 4) * X + q // 4, sub

    def to_ring(r):
        return (r * 4 + low) * X + x, sub

    def to_x(p):
        return z * X + p, sub

    def to_z(p):
        return p * X + x, sub

    def copy(src, dst, send, recv, where):
        return pltpu.make_async_remote_copy(
            src_ref=src, dst_ref=dst, send_sem=send, recv_sem=recv, device_id=where, device_id_type=MESH)

    def peers(n, me):
        def wrap(body):
            def step(i, carry):
                body(lax.rem(me + i, n))
                return carry
            lax.fori_loop(1, n, step, 0)
        return wrap

    def far_first(n, me):
        def wrap(body):
            def step(i, carry):
                body(lax.rem(me + n // 2 + (1 - 2 * (i % 2)) * ((i + 1) // 2), n))
                return carry
            lax.fori_loop(0, n - 1, step, 0)
        return wrap

    loads = [
        pltpu.make_async_copy(cand_hbm, cand, s_in.at[0]),
        pltpu.make_async_copy(pts_hbm, pts.at[sub], s_in.at[1]),
        pltpu.make_async_copy(owner_hbm, owner, s_in.at[2]),
    ]
    for load in loads:
        load.start()

    barrier = pltpu.get_barrier_semaphore()
    for order, n, me, to in ((far_first, Z, z, to_z), (peers, Q, q_me, to_plane), (peers, MEMBERS, sub, to_member)):
        @order(n, me)
        def _(p, to=to):
            pl.semaphore_signal(barrier, inc=1, device_id=to(p), device_id_type=MESH)

    loads[0].wait()

    step = 64
    hits = []
    for lo in range(0, n_pts, step):
        local = iota((step, 128), 0) + (device * n_pts + lo)
        hit = jnp.zeros((step, 128), F32)
        for rnd in range(rounds):
            for t in range(tiles):
                hit = jnp.where(local == cand[rnd:rnd + 1, 128 * t:128 * (t + 1)], 1.0, hit)
        hits.append(jnp.max(hit, axis=1, keepdims=True))
    hit = jnp.concatenate(hits, axis=0)
    below = jnp.where(iota((n_pts, n_pts), 1) < iota((n_pts, n_pts), 0), 1.0, 0.0).astype(BF16)
    rank = jnp.dot(below, jnp.broadcast_to(hit, (n_pts, 128)).astype(BF16), preferred_element_type=F32)
    rank = rank.astype(jnp.int32)
    lane = iota((n_pts, 128), 1)
    sel = jnp.where((rank == lane) & (lane < SLOTS), hit, 0.0).astype(BF16)
    loads[1].wait()
    picked = lax.dot_general(sel, pts[sub], (((0,), (0,)), ((), ())), preferred_element_type=F32)
    moved = jnp.where(rank + (sub % 4) * SLOTS == lane, hit, 0.0)
    rowno = iota((n_pts, 128), 0)
    upper = jnp.sum(moved * (rowno >> 1).astype(F32), axis=0, keepdims=True)
    lower = jnp.sum(moved * (rowno & 1).astype(F32), axis=0, keepdims=True)
    used = jnp.sum(moved, axis=0, keepdims=True)
    which = iota((16, 128), 0)
    ids = jnp.where(which == 0, upper, jnp.where(which == 1, lower, jnp.where(which == 2, used, 0.0)))
    pack[0:SLOTS, :] = picked[0:SLOTS, 0:128].astype(BF16)
    pack[SLOTS:2 * SLOTS, :] = picked[0:SLOTS, 128:256].astype(BF16)
    pack[2 * SLOTS:2 * SLOTS + 16, :] = ids.astype(BF16)
    packs[sub] = pack[...]

    pl.semaphore_wait(barrier, MEMBERS + Q + Z - 3)

    @far_first(MEMBERS, sub)
    def _(p):
        copy(pack, packs.at[sub], s_pack.at[p], r_pack.at[sub], to_member(p)).start()

    loads[2].wait()

    for blk in range(rows // 128):
        i = iota((128, 128), 0) + 128 * blk
        group = (i * 10923) >> 16
        q, r, j = group >> 2, group & 3, i - group * OUT_ROWS
        slot = ((((r << 2) + (q & 3)) * X + (q >> 2)) * MEMBERS + sub) * OUT_ROWS + j
        found = jnp.zeros((128, 128), F32)
        for rnd in range(rounds):
            for t in range(tiles):
                c = cand[rnd:rnd + 1, 128 * t:128 * (t + 1)].astype(F32)
                o = owner[rnd * tiles + t:rnd * tiles + t + 1, :]
                found = jnp.where(slot == o, c, found)
        target[128 * blk:128 * (blk + 1), :] = jnp.broadcast_to(
            jnp.sum(found, axis=1, keepdims=True), (128, 128))

    @peers(MEMBERS, sub)
    def _(p):
        copy(pack, packs.at[p], s_pack.at[p], r_pack.at[p], to_member(p)).wait_recv()

    hots = []
    for half in range(2):
        ident = jnp.zeros((1, 128), F32)
        for m in range(4 * half, 4 * half + 4):
            tile = packs[m, 2 * SLOTS:2 * SLOTS + 16, :].astype(F32)
            first = ((dp * MEMBERS + m) * n_pts + 1).astype(F32)
            ident = ident + 2.0 * tile[0:1, :] + tile[1:2, :] + first * tile[2:3, :]
        hots.append(jnp.where(target[...] + 1.0 == ident, 1.0, 0.0).astype(BF16))
    hot = jnp.concatenate(hots, axis=1)
    left = jnp.dot(hot, packs[:, 0:SLOTS, :].reshape(MEMBERS * SLOTS, 128), preferred_element_type=F32)
    right = jnp.dot(hot, packs[:, SLOTS:2 * SLOTS, :].reshape(MEMBERS * SLOTS, 128), preferred_element_type=F32)
    for q in range(Q):
        both = jnp.concatenate([left[per_q * q:per_q * (q + 1)], right[per_q * q:per_q * (q + 1)]], axis=0)
        dense[q] = both.astype(BF16)

    @far_first(Q, q_me)
    def _(p):
        copy(dense.at[p], drecv.at[q_me], s_d.at[p], r_d.at[q_me], to_plane(p)).start()

    @peers(CHIPS, chip)
    def _(p):
        copy(pts.at[sub], pts.at[sub], s_pts.at[p], r_pts.at[chip], to_chip(p)).start()

    copy(pts.at[sub], pts.at[sub], s_sib.at[chip], r_sib.at[chip], sibling).start()

    psum[...] = dense[q_me].astype(F32)

    @far_first(Q, q_me)
    def _(p):
        copy(dense.at[p], drecv.at[p], s_d.at[p], r_d.at[p], to_plane(p)).wait_recv()
        psum[...] += drecv[p].astype(F32)

    rsend[...] = psum[...].astype(BF16)

    @far_first(R, high)
    def _(p):
        copy(rsend, rrecv.at[high], s_r.at[p], r_r.at[high], to_ring(p)).start()

    @far_first(R, high)
    def _(p):
        copy(rsend, rrecv.at[p], s_r.at[p], r_r.at[p], to_ring(p)).wait_recv()
        psum[...] += rrecv[p].astype(F32)

    csend[...] = psum[...].astype(BF16)

    def wide_peers(b):
        def wrap(body):
            def step(i, carry):
                body(lax.rem(x + b, X) * 4 + lax.rem(low + i, 4))
                return carry
            lax.fori_loop(0 if b else 1, 4, step, 0)
        return wrap

    for b in (2, 3, 1, 0):
        @wide_peers(b)
        def _(p):
            copy(csend, c_buf.at[q_me], s_c.at[p], r_c.at[q_me], to_plane(p)).start()

    c_buf[q_me] = csend[...]

    @peers(CHIPS, chip)
    def _(p):
        slot = pts.at[p * CORES + core]
        copy(slot, slot, s_pts.at[p], r_pts.at[p], to_chip(p)).wait_recv()
        copy(slot, slot, s_sib.at[p], r_sib.at[p], sibling).start()

    nt = (((1,), (1,)), ((), ()))

    def norms(idx):
        wide = pts[idx].astype(F32)
        square = wide * wide
        top = square.astype(BF16)
        rest = (square - top.astype(F32)).astype(BF16)
        ones = jnp.ones((8, wide.shape[1]), BF16)
        pn = (lax.dot_general(ones, top, nt, preferred_element_type=F32)
              + lax.dot_general(ones, rest, nt, preferred_element_type=F32))
        pn_buf[idx] = pn[0:1, :]

    @peers(CHIPS + 1, 0)
    def _(i):
        norms(lax.rem(chip + i, CHIPS) * CORES + core)

    @peers(CHIPS + 1, 0)
    def _(i):
        p = lax.rem(chip + i, CHIPS)
        slot = pts.at[p * CORES + 1 - core]
        copy(slot, slot, s_sib.at[p], r_sib.at[p], sibling).wait_recv()
        norms(p * CORES + 1 - core)

    diag = iota((per_q, 128), 0) == iota((per_q, 128), 1)
    highest = []
    for pair in ((2, 1), (3, 0)):
        lefts, rights = [], []
        for b in pair:
            @wide_peers(b)
            def _(p):
                copy(csend, c_buf.at[p], s_c.at[p], r_c.at[p], to_plane(p)).wait_recv()

            for l in range(4):
                rows_q = c_buf[lax.rem(x + b, X) * 4 + l].astype(F32)
                lefts.append(rows_q[0:per_q])
                rights.append(rows_q[per_q:2 * per_q])
        chosen = jnp.concatenate([jnp.concatenate(lefts, axis=0), jnp.concatenate(rights, axis=0)], axis=1)
        cn = jnp.sum(chosen * chosen, axis=1, keepdims=True)
        twice = (2.0 * chosen).astype(BF16)
        weights, peaks, mass = [], [], None
        for m in range(MEMBERS):
            dots = lax.dot_general(twice, pts[m], nt, preferred_element_type=F32)
            less = dots - cn
            peaks.append(jnp.max(less, axis=0, keepdims=True))
            weight = jnp.exp2((less - pn_buf[m]) * SCALE).astype(BF16)
            weights.append(weight)
            wide_w = weight.astype(F32)
            for t in range(n_pts // 128):
                piece = wide_w[:, 128 * t:128 * (t + 1)]
                mass = piece if mass is None else mass + piece
        sums = jnp.dot(jnp.concatenate(weights, axis=1), pts[...].reshape(MEMBERS * n_pts, -1),
                       preferred_element_type=F32)
        highest.append(peaks)
        total = jnp.sum(mass, axis=1, keepdims=True)
        for l in range(4):
            for k, b in enumerate(pair):
                dest = fsend.at[b, l]
                lo = per_x * k + per_q * l
                dest[0:per_q, :] = sums[lo:lo + per_q, 0:128]
                dest[per_q:2 * per_q, :] = sums[lo:lo + per_q, 128:256]
                line = jnp.sum(jnp.where(diag, total[lo:lo + per_q], 0.0), axis=0, keepdims=True)
                dest[2 * per_q:PIECE, :] = line
                if b:
                    p = lax.rem(x + b, X)
                    copy(dest.at[0:PIECE], frecv.at[x, l, 0:PIECE], s_f.at[p, l], r_f.at[x, l], to_x(p)).start()

    for l in range(4):
        part = fsend[0, l, 0:PIECE]
        for b in (1, 2, 3):
            p = lax.rem(x + b, X)
            piece = frecv.at[p, l, 0:PIECE]
            copy(piece, piece, s_f.at[p, l], r_f.at[p, l], sibling).wait_recv()
            part = part + piece[...]
        fsum[l, 0:PIECE, :] = part
        for r in range(R):
            p = r * 4 + l
            lo = OUT_ROWS * r
            gsend[p, 0:OUT_ROWS, :] = fsum[l, lo:lo + OUT_ROWS, :]
            gsend[p, OUT_ROWS:OUT_ROWS + 1, :] = fsum[l, 2 * per_q:2 * per_q + 1, :]
            gsend[p, OUT_ROWS + 1:PACKED, :] = fsum[l, per_q + lo:per_q + lo + OUT_ROWS, :]

            @pl.when(p != z)
            def _():
                copy(gsend.at[p, 0:PACKED], grecv.at[z, 0:PACKED], s_g.at[p], r_g.at[z], to_z(p)).start()

    for m in range(MEMBERS):
        near = pn_buf[m] - jnp.maximum(highest[0][m], highest[1][m])
        for t in range(n_pts // 128):
            minsend[m, t:t + 1, :] = near[:, 128 * t:128 * (t + 1)]

    @peers(MEMBERS, sub)
    def _(p):
        copy(minsend.at[p], minrecv.at[sub], s_m.at[p], r_m.at[sub], to_member(p)).start()

    @peers(MEMBERS, sub)
    def _(p):
        copy(pack, packs.at[sub], s_pack.at[p], r_pack.at[p], to_member(p)).wait_send()

    @peers(CHIPS, chip)
    def _(p):
        slot = pts.at[p * CORES + core]
        copy(slot, slot, s_pts.at[p], r_pts.at[p], sibling).wait_send()
        copy(slot, slot, s_sib.at[p], r_sib.at[p], sibling).wait_send()

    copy(pts.at[sub], pts.at[sub], s_sib.at[chip], r_sib.at[chip], sibling).wait_send()

    @peers(Q, q_me)
    def _(p):
        copy(dense.at[p], drecv.at[p], s_d.at[p], r_d.at[p], sibling).wait_send()

    @peers(Q, q_me)
    def _(p):
        copy(csend, c_buf.at[p], s_c.at[p], r_c.at[p], sibling).wait_send()

    @peers(R, high)
    def _(p):
        copy(rsend, rrecv.at[p], s_r.at[p], r_r.at[p], sibling).wait_send()

    @peers(X, x)
    def _(p):
        for l in range(4):
            piece = frecv.at[p, l, 0:PIECE]
            copy(piece, piece, s_f.at[p, l], r_f.at[p, l], sibling).wait_send()

    out_min[...] = minsend[sub]

    @peers(MEMBERS, sub)
    def _(p):
        copy(minsend.at[p], minrecv.at[p], s_m.at[p], r_m.at[p], to_member(p)).wait_recv()
        out_min[...] = jnp.minimum(out_min[...], minrecv[p])

    @peers(MEMBERS, sub)
    def _(p):
        copy(minsend.at[p], minrecv.at[p], s_m.at[p], r_m.at[p], to_member(p)).wait_send()

    final = fsum.at[0, 0:16]
    final[0:PACKED, :] = gsend[z, 0:PACKED, :]

    @peers(Z, z)
    def _(p):
        piece = grecv.at[p, 0:PACKED]
        copy(piece, piece, s_g.at[p], r_g.at[p], to_z(p)).wait_send()

    @peers(Z, z)
    def _(p):
        piece = grecv.at[p, 0:PACKED]
        copy(piece, piece, s_g.at[p], r_g.at[p], to_z(p)).wait_recv()
        final[0:PACKED, :] += piece[...]

    out_sums[...] = final[...]


def finish(sums, near, out_cent, out_mass, out_min):
    high = lax.axis_index("dp") // X // 4
    line = sums[OUT_ROWS:OUT_ROWS + 1, :]
    pick = iota((8, 128), 1) == iota((8, 128), 0) + OUT_ROWS * high
    column = jnp.sum(jnp.where(pick, line, 0.0), axis=1, keepdims=True)
    out_cent[:, 0:128] = sums[0:OUT_ROWS, :] / column[0:OUT_ROWS]
    out_cent[:, 128:256] = sums[OUT_ROWS + 1:PACKED, :] / column[0:OUT_ROWS]
    eye = iota((8, 128), 1) == iota((8, 128), 0)
    out_mass[...] = jnp.sum(jnp.where(eye, column, 0.0), axis=0, keepdims=True)[:, 0:OUT_ROWS]
    out_min[...] = near[...]


def on_device(points, candidates, owner_slot):
    n_pts, dim = points.shape
    per_q, per_x = R * OUT_ROWS, Z * OUT_ROWS
    rows = Q * per_q
    owner = owner_slot.reshape(-1, 128)
    vmem = pltpu.VMEM
    dma = pltpu.SemaphoreType.DMA
    scratch = [
        vmem((MEMBERS, n_pts, dim), BF16),
        vmem(candidates.shape, jnp.int32),
        vmem(owner.shape, jnp.int32),
        vmem((2 * SLOTS + 16, 128), BF16),
        vmem((MEMBERS, 2 * SLOTS + 16, 128), BF16),
        vmem((rows, 128), F32),
        vmem((Q, 2 * per_q, 128), BF16),
        vmem((Q, 2 * per_q, 128), BF16),
        vmem((2 * per_q, 128), F32),
        vmem((2 * per_q, 128), BF16),
        vmem((R, 2 * per_q, 128), BF16),
        vmem((2 * per_q, 128), BF16),
        vmem((Q, 2 * per_q, 128), BF16),
        vmem((MEMBERS, 1, n_pts), F32),
        vmem((MEMBERS, n_pts // 128, 128), F32),
        vmem((MEMBERS, n_pts // 128, 128), F32),
        vmem((X, 4, 2 * per_q + 8, 128), F32),
        vmem((X, 4, 2 * per_q + 8, 128), F32),
        vmem((4, 2 * per_q + 8, 128), F32),
        vmem((Z, 16, 128), F32),
        vmem((Z, 16, 128), F32),
        dma((3,)),
    ]
    for n in ((MEMBERS,), (CHIPS,), (CHIPS,), (Q,), (R,), (Q,), (X, 4), (Z,), (MEMBERS,)):
        scratch += [dma(n), dma(n)]
    sums, near = pl.pallas_call(
        kernel,
        out_shape=(
            jax.ShapeDtypeStruct((16, 128), F32),
            jax.ShapeDtypeStruct((n_pts // 128, 128), F32),
        ),
        in_specs=[pl.BlockSpec(memory_space=pltpu.HBM)] * 3,
        out_specs=[pl.BlockSpec(memory_space=vmem)] * 2,
        scratch_shapes=scratch,
        compiler_params=pltpu.CompilerParams(
            collective_id=0, has_side_effects=True, vmem_limit_bytes=55213 * 2 ** 10),
    )(points, candidates, owner)
    cent, mass, near = pl.pallas_call(
        finish,
        out_shape=(
            jax.ShapeDtypeStruct((OUT_ROWS, dim), F32),
            jax.ShapeDtypeStruct((1, OUT_ROWS), F32),
            jax.ShapeDtypeStruct((n_pts // 128, 128), F32),
        ),
        in_specs=[pl.BlockSpec(memory_space=vmem)] * 2,
        out_specs=[pl.BlockSpec(memory_space=vmem)] * 3,
        compiler_params=pltpu.CompilerParams(vmem_limit_bytes=2 ** 20),
    )(sums, near)
    return cent, mass.reshape(-1), near.reshape(-1)


def solution(mesh):
    return jax.shard_map(
        on_device,
        mesh=mesh,
        in_specs=(P(("dp", "sub"), None), P(), P()),
        out_specs=(P(("dp", "sub"), None), P(("dp", "sub")), P(("dp", "sub"))),
        check_vma=False,
    )
```

```python
import math

import jax
import jax.numpy as jnp
from jax import lax
from jax.experimental import pallas as pl
from jax.experimental.pallas import tpu as pltpu
from jax.sharding import PartitionSpec as P

MESH = pl.DeviceIdType.MESH
F32 = jnp.float32
BF16 = jnp.bfloat16
CORES = 2
CHIPS = 4
MEMBERS = CHIPS * CORES
OUT_ROWS = 6
SLOTS = 32
SCALE = 4.0 * math.log2(math.e)


Q, R = 16, 4
X, Z = 4, 16
PIECE = 2 * R * OUT_ROWS + 1
PACKED = 2 * OUT_ROWS + 1


def iota(shape, dim):
    return lax.broadcasted_iota(jnp.int32, shape, dim)


def kernel(pts_hbm, cand_hbm, owner_hbm, out_sums, out_min,
           pts, cand, owner, pack, packs, target, dense, drecv, psum, rsend, rrecv, csend, c_buf,
           pn_buf, minsend, minrecv, fsend, frecv, fsum, gsend, grecv,
           s_in, s_pack, r_pack, s_pts, r_pts, s_sib, r_sib, s_d, r_d, s_r, r_r, s_c, r_c,
           s_f, r_f, s_g, r_g, s_m, r_m):
    per_q = R * OUT_ROWS
    per_x = Z * OUT_ROWS
    rows = Q * per_q
    n_pts = pts_hbm.shape[0]
    rounds, per_round = cand.shape
    tiles = per_round // 128
    dp, sub = lax.axis_index("dp"), lax.axis_index("sub")
    z, x, chip, core = dp // X, dp % X, sub // CORES, sub % CORES
    low, high = z % 4, z // 4
    q_me = x * 4 + low
    device = dp * MEMBERS + sub
    sibling = (dp, chip * CORES + 1 - core)

    def to_member(m):
        return dp, m

    def to_chip(p):
        return dp, p * CORES + core

    def to_plane(q):
        return (high * 4 + q % 4) * X + q // 4, sub

    def to_ring(r):
        return (r * 4 + low) * X + x, sub

    def to_x(p):
        return z * X + p, sub

    def to_z(p):
        return p * X + x, sub

    def copy(src, dst, send, recv, where):
        return pltpu.make_async_remote_copy(
            src_ref=src, dst_ref=dst, send_sem=send, recv_sem=recv, device_id=where, device_id_type=MESH)

    def peers(n, me):
        def wrap(body):
            def step(i, carry):
                body(lax.rem(me + i, n))
                return carry
            lax.fori_loop(1, n, step, 0)
        return wrap

    def far_first(n, me):
        def wrap(body):
            def step(i, carry):
                body(lax.rem(me + n // 2 + (1 - 2 * (i % 2)) * ((i + 1) // 2), n))
                return carry
            lax.fori_loop(0, n - 1, step, 0)
        return wrap

    loads = [
        pltpu.make_async_copy(cand_hbm, cand, s_in.at[0]),
        pltpu.make_async_copy(pts_hbm, pts.at[sub], s_in.at[1]),
        pltpu.make_async_copy(owner_hbm, owner, s_in.at[2]),
    ]
    for load in loads:
        load.start()

    barrier = pltpu.get_barrier_semaphore()
    for order, n, me, to in ((far_first, Z, z, to_z), (peers, Q, q_me, to_plane), (peers, MEMBERS, sub, to_member)):
        @order(n, me)
        def _(p, to=to):
            pl.semaphore_signal(barrier, inc=1, device_id=to(p), device_id_type=MESH)

    loads[0].wait()

    step = 64
    hits = []
    for lo in range(0, n_pts, step):
        local = iota((step, 128), 0) + (device * n_pts + lo)
        hit = jnp.zeros((step, 128), F32)
        for rnd in range(rounds):
            for t in range(tiles):
                hit = jnp.where(local == cand[rnd:rnd + 1, 128 * t:128 * (t + 1)], 1.0, hit)
        hits.append(jnp.max(hit, axis=1, keepdims=True))
    hit = jnp.concatenate(hits, axis=0)
    below = jnp.where(iota((n_pts, n_pts), 1) < iota((n_pts, n_pts), 0), 1.0, 0.0).astype(BF16)
    rank = jnp.dot(below, jnp.broadcast_to(hit, (n_pts, 128)).astype(BF16), preferred_element_type=F32)
    rank = rank.astype(jnp.int32)
    lane = iota((n_pts, 128), 1)
    sel = jnp.where((rank == lane) & (lane < SLOTS), hit, 0.0).astype(BF16)
    loads[1].wait()
    picked = lax.dot_general(sel, pts[sub], (((0,), (0,)), ((), ())), preferred_element_type=F32)
    moved = jnp.where(rank + (sub % 4) * SLOTS == lane, hit, 0.0)
    rowno = iota((n_pts, 128), 0)
    upper = jnp.sum(moved * (rowno >> 1).astype(F32), axis=0, keepdims=True)
    lower = jnp.sum(moved * (rowno & 1).astype(F32), axis=0, keepdims=True)
    used = jnp.sum(moved, axis=0, keepdims=True)
    which = iota((16, 128), 0)
    ids = jnp.where(which == 0, upper, jnp.where(which == 1, lower, jnp.where(which == 2, used, 0.0)))
    pack[0:SLOTS, :] = picked[0:SLOTS, 0:128].astype(BF16)
    pack[SLOTS:2 * SLOTS, :] = picked[0:SLOTS, 128:256].astype(BF16)
    pack[2 * SLOTS:2 * SLOTS + 16, :] = ids.astype(BF16)
    packs[sub] = pack[...]

    pl.semaphore_wait(barrier, MEMBERS + Q + Z - 3)

    @far_first(MEMBERS, sub)
    def _(p):
        copy(pack, packs.at[sub], s_pack.at[p], r_pack.at[sub], to_member(p)).start()

    loads[2].wait()

    for blk in range(rows // 128):
        i = iota((128, 128), 0) + 128 * blk
        group = (i * 10923) >> 16
        q, r, j = group >> 2, group & 3, i - group * OUT_ROWS
        slot = ((((r << 2) + (q & 3)) * X + (q >> 2)) * MEMBERS + sub) * OUT_ROWS + j
        found = jnp.zeros((128, 128), F32)
        for rnd in range(rounds):
            for t in range(tiles):
                c = cand[rnd:rnd + 1, 128 * t:128 * (t + 1)].astype(F32)
                o = owner[rnd * tiles + t:rnd * tiles + t + 1, :]
                found = jnp.where(slot == o, c, found)
        target[128 * blk:128 * (blk + 1), :] = jnp.broadcast_to(
            jnp.sum(found, axis=1, keepdims=True), (128, 128))

    @peers(MEMBERS, sub)
    def _(p):
        copy(pack, packs.at[p], s_pack.at[p], r_pack.at[p], to_member(p)).wait_recv()

    hots = []
    for half in range(2):
        ident = jnp.zeros((1, 128), F32)
        for m in range(4 * half, 4 * half + 4):
            tile = packs[m, 2 * SLOTS:2 * SLOTS + 16, :].astype(F32)
            first = ((dp * MEMBERS + m) * n_pts + 1).astype(F32)
            ident = ident + 2.0 * tile[0:1, :] + tile[1:2, :] + first * tile[2:3, :]
        hots.append(jnp.where(target[...] + 1.0 == ident, 1.0, 0.0).astype(BF16))
    hot = jnp.concatenate(hots, axis=1)
    left = jnp.dot(hot, packs[:, 0:SLOTS, :].reshape(MEMBERS * SLOTS, 128), preferred_element_type=F32)
    right = jnp.dot(hot, packs[:, SLOTS:2 * SLOTS, :].reshape(MEMBERS * SLOTS, 128), preferred_element_type=F32)
    for q in range(Q):
        both = jnp.concatenate([left[per_q * q:per_q * (q + 1)], right[per_q * q:per_q * (q + 1)]], axis=0)
        dense[q] = both.astype(BF16)

    @far_first(Q, q_me)
    def _(p):
        copy(dense.at[p], drecv.at[q_me], s_d.at[p], r_d.at[q_me], to_plane(p)).start()

    @peers(CHIPS, chip)
    def _(p):
        copy(pts.at[sub], pts.at[sub], s_pts.at[p], r_pts.at[chip], to_chip(p)).start()

    copy(pts.at[sub], pts.at[sub], s_sib.at[chip], r_sib.at[chip], sibling).start()

    psum[...] = dense[q_me].astype(F32)

    @far_first(Q, q_me)
    def _(p):
        copy(dense.at[p], drecv.at[p], s_d.at[p], r_d.at[p], to_plane(p)).wait_recv()
        psum[...] += drecv[p].astype(F32)

    rsend[...] = psum[...].astype(BF16)

    @far_first(R, high)
    def _(p):
        copy(rsend, rrecv.at[high], s_r.at[p], r_r.at[high], to_ring(p)).start()

    @far_first(R, high)
    def _(p):
        copy(rsend, rrecv.at[p], s_r.at[p], r_r.at[p], to_ring(p)).wait_recv()
        psum[...] += rrecv[p].astype(F32)

    csend[...] = psum[...].astype(BF16)

    def wide_peers(b):
        def wrap(body):
            def step(i, carry):
                body(lax.rem(x + b, X) * 4 + lax.rem(low + i, 4))
                return carry
            lax.fori_loop(0 if b else 1, 4, step, 0)
        return wrap

    for b in (2, 3, 1, 0):
        @wide_peers(b)
        def _(p):
            copy(csend, c_buf.at[q_me], s_c.at[p], r_c.at[q_me], to_plane(p)).start()

    c_buf[q_me] = csend[...]

    @peers(CHIPS, chip)
    def _(p):
        slot = pts.at[p * CORES + core]
        copy(slot, slot, s_pts.at[p], r_pts.at[p], to_chip(p)).wait_recv()
        copy(slot, slot, s_sib.at[p], r_sib.at[p], sibling).start()

    nt = (((1,), (1,)), ((), ()))

    def norms(idx):
        wide = pts[idx].astype(F32)
        square = wide * wide
        top = square.astype(BF16)
        wide_top = top.astype(F32)
        rest = jnp.where(wide_top == square, 0.0, square - wide_top).astype(BF16)
        ones = jnp.ones((8, wide.shape[1]), BF16)
        pn = (lax.dot_general(ones, top, nt, preferred_element_type=F32)
              + lax.dot_general(ones, rest, nt, preferred_element_type=F32))
        pn_buf[idx] = pn[0:1, :]

    @peers(CHIPS + 1, 0)
    def _(i):
        norms(lax.rem(chip + i, CHIPS) * CORES + core)

    @peers(CHIPS + 1, 0)
    def _(i):
        p = lax.rem(chip + i, CHIPS)
        slot = pts.at[p * CORES + 1 - core]
        copy(slot, slot, s_sib.at[p], r_sib.at[p], sibling).wait_recv()
        norms(p * CORES + 1 - core)

    diag = iota((per_q, 128), 0) == iota((per_q, 128), 1)
    highest = []
    for group in ((2, 1), (3,), (0,)):
        lefts, rights = [], []
        for b in group:
            @wide_peers(b)
            def _(p):
                copy(csend, c_buf.at[p], s_c.at[p], r_c.at[p], to_plane(p)).wait_recv()

            for l in range(4):
                rows_q = c_buf[lax.rem(x + b, X) * 4 + l].astype(F32)
                lefts.append(rows_q[0:per_q])
                rights.append(rows_q[per_q:2 * per_q])
        chosen = jnp.concatenate([jnp.concatenate(lefts, axis=0), jnp.concatenate(rights, axis=0)], axis=1)
        cn = jnp.sum(chosen * chosen, axis=1, keepdims=True)
        twice = (2.0 * chosen).astype(BF16)
        weights, peaks, mass = [], [], None
        for m in range(MEMBERS):
            dots = lax.dot_general(twice, pts[m], nt, preferred_element_type=F32)
            less = dots - cn
            peaks.append(jnp.max(less, axis=0, keepdims=True))
            weight = jnp.exp2((less - pn_buf[m]) * SCALE).astype(BF16)
            weights.append(weight)
            wide_w = weight.astype(F32)
            for t in range(n_pts // 128):
                piece = wide_w[:, 128 * t:128 * (t + 1)]
                mass = piece if mass is None else mass + piece
        sums = jnp.dot(jnp.concatenate(weights, axis=1), pts[...].reshape(MEMBERS * n_pts, -1),
                       preferred_element_type=F32)
        highest.append(peaks)
        total = jnp.sum(mass, axis=1, keepdims=True)
        for l in range(4):
            for k, b in enumerate(group):
                dest = fsend.at[b, l]
                lo = per_x * k + per_q * l
                dest[0:per_q, :] = sums[lo:lo + per_q, 0:128]
                dest[per_q:2 * per_q, :] = sums[lo:lo + per_q, 128:256]
                line = jnp.sum(jnp.where(diag, total[lo:lo + per_q], 0.0), axis=0, keepdims=True)
                dest[2 * per_q:PIECE, :] = line
                if b:
                    p = lax.rem(x + b, X)
                    copy(dest.at[0:PIECE], frecv.at[x, l, 0:PIECE], s_f.at[p, l], r_f.at[x, l], to_x(p)).start()

    for l in range(4):
        part = fsend[0, l, 0:PIECE]
        for b in (1, 2, 3):
            p = lax.rem(x + b, X)
            piece = frecv.at[p, l, 0:PIECE]
            copy(piece, piece, s_f.at[p, l], r_f.at[p, l], sibling).wait_recv()
            part = part + piece[...]
        fsum[l, 0:PIECE, :] = part
        for r in range(R):
            p = r * 4 + l
            lo = OUT_ROWS * r
            gsend[p, 0:OUT_ROWS, :] = fsum[l, lo:lo + OUT_ROWS, :]
            gsend[p, OUT_ROWS:OUT_ROWS + 1, :] = fsum[l, 2 * per_q:2 * per_q + 1, :]
            gsend[p, OUT_ROWS + 1:PACKED, :] = fsum[l, per_q + lo:per_q + lo + OUT_ROWS, :]

            @pl.when(p != z)
            def _():
                copy(gsend.at[p, 0:PACKED], grecv.at[z, 0:PACKED], s_g.at[p], r_g.at[z], to_z(p)).start()

    for m in range(MEMBERS):
        peak = highest[0][m]
        for other in highest[1:]:
            peak = jnp.maximum(peak, other[m])
        near = pn_buf[m] - peak
        for t in range(n_pts // 128):
            minsend[m, t:t + 1, :] = near[:, 128 * t:128 * (t + 1)]

    @far_first(MEMBERS, sub)
    def _(p):
        copy(minsend.at[p], minrecv.at[sub], s_m.at[p], r_m.at[sub], to_member(p)).start()

    @peers(MEMBERS, sub)
    def _(p):
        copy(pack, packs.at[sub], s_pack.at[p], r_pack.at[p], to_member(p)).wait_send()

    @peers(CHIPS, chip)
    def _(p):
        slot = pts.at[p * CORES + core]
        copy(slot, slot, s_pts.at[p], r_pts.at[p], sibling).wait_send()
        copy(slot, slot, s_sib.at[p], r_sib.at[p], sibling).wait_send()

    copy(pts.at[sub], pts.at[sub], s_sib.at[chip], r_sib.at[chip], sibling).wait_send()

    @peers(Q, q_me)
    def _(p):
        copy(dense.at[p], drecv.at[p], s_d.at[p], r_d.at[p], sibling).wait_send()

    @peers(Q, q_me)
    def _(p):
        copy(csend, c_buf.at[p], s_c.at[p], r_c.at[p], sibling).wait_send()

    @peers(R, high)
    def _(p):
        copy(rsend, rrecv.at[p], s_r.at[p], r_r.at[p], sibling).wait_send()

    @peers(X, x)
    def _(p):
        for l in range(4):
            piece = frecv.at[p, l, 0:PIECE]
            copy(piece, piece, s_f.at[p, l], r_f.at[p, l], sibling).wait_send()

    out_min[...] = minsend[sub]

    @peers(MEMBERS, sub)
    def _(p):
        copy(minsend.at[p], minrecv.at[p], s_m.at[p], r_m.at[p], to_member(p)).wait_recv()
        out_min[...] = jnp.minimum(out_min[...], minrecv[p])

    @peers(MEMBERS, sub)
    def _(p):
        copy(minsend.at[p], minrecv.at[p], s_m.at[p], r_m.at[p], to_member(p)).wait_send()

    final = fsum.at[0, 0:16]
    final[0:PACKED, :] = gsend[z, 0:PACKED, :]

    @peers(Z, z)
    def _(p):
        piece = grecv.at[p, 0:PACKED]
        copy(piece, piece, s_g.at[p], r_g.at[p], to_z(p)).wait_send()

    @peers(Z, z)
    def _(p):
        piece = grecv.at[p, 0:PACKED]
        copy(piece, piece, s_g.at[p], r_g.at[p], to_z(p)).wait_recv()
        final[0:PACKED, :] += piece[...]

    out_sums[...] = final[...]


def finish(sums, near, out_cent, out_mass, out_min):
    high = lax.axis_index("dp") // X // 4
    line = sums[OUT_ROWS:OUT_ROWS + 1, :]
    pick = iota((8, 128), 1) == iota((8, 128), 0) + OUT_ROWS * high
    column = jnp.sum(jnp.where(pick, line, 0.0), axis=1, keepdims=True)
    out_cent[:, 0:128] = sums[0:OUT_ROWS, :] / column[0:OUT_ROWS]
    out_cent[:, 128:256] = sums[OUT_ROWS + 1:PACKED, :] / column[0:OUT_ROWS]
    eye = iota((8, 128), 1) == iota((8, 128), 0)
    out_mass[...] = jnp.sum(jnp.where(eye, column, 0.0), axis=0, keepdims=True)[:, 0:OUT_ROWS]
    out_min[...] = near[...]


def on_device(points, candidates, owner_slot):
    n_pts, dim = points.shape
    per_q, per_x = R * OUT_ROWS, Z * OUT_ROWS
    rows = Q * per_q
    owner = owner_slot.reshape(-1, 128)
    vmem = pltpu.VMEM
    dma = pltpu.SemaphoreType.DMA
    scratch = [
        vmem((MEMBERS, n_pts, dim), BF16),
        vmem(candidates.shape, jnp.int32),
        vmem(owner.shape, jnp.int32),
        vmem((2 * SLOTS + 16, 128), BF16),
        vmem((MEMBERS, 2 * SLOTS + 16, 128), BF16),
        vmem((rows, 128), F32),
        vmem((Q, 2 * per_q, 128), BF16),
        vmem((Q, 2 * per_q, 128), BF16),
        vmem((2 * per_q, 128), F32),
        vmem((2 * per_q, 128), BF16),
        vmem((R, 2 * per_q, 128), BF16),
        vmem((2 * per_q, 128), BF16),
        vmem((Q, 2 * per_q, 128), BF16),
        vmem((MEMBERS, 1, n_pts), F32),
        vmem((MEMBERS, n_pts // 128, 128), F32),
        vmem((MEMBERS, n_pts // 128, 128), F32),
        vmem((X, 4, 2 * per_q + 8, 128), F32),
        vmem((X, 4, 2 * per_q + 8, 128), F32),
        vmem((4, 2 * per_q + 8, 128), F32),
        vmem((Z, 16, 128), F32),
        vmem((Z, 16, 128), F32),
        dma((3,)),
    ]
    for n in ((MEMBERS,), (CHIPS,), (CHIPS,), (Q,), (R,), (Q,), (X, 4), (Z,), (MEMBERS,)):
        scratch += [dma(n), dma(n)]
    sums, near = pl.pallas_call(
        kernel,
        out_shape=(
            jax.ShapeDtypeStruct((16, 128), F32),
            jax.ShapeDtypeStruct((n_pts // 128, 128), F32),
        ),
        in_specs=[pl.BlockSpec(memory_space=pltpu.HBM)] * 3,
        out_specs=[pl.BlockSpec(memory_space=vmem)] * 2,
        scratch_shapes=scratch,
        compiler_params=pltpu.CompilerParams(
            collective_id=0, has_side_effects=True, vmem_limit_bytes=55213 * 2 ** 10),
    )(points, candidates, owner)
    cent, mass, near = pl.pallas_call(
        finish,
        out_shape=(
            jax.ShapeDtypeStruct((OUT_ROWS, dim), F32),
            jax.ShapeDtypeStruct((1, OUT_ROWS), F32),
            jax.ShapeDtypeStruct((n_pts // 128, 128), F32),
        ),
        in_specs=[pl.BlockSpec(memory_space=vmem)] * 2,
        out_specs=[pl.BlockSpec(memory_space=vmem)] * 3,
        compiler_params=pltpu.CompilerParams(vmem_limit_bytes=2 ** 20),
    )(sums, near)
    return cent, mass.reshape(-1), near.reshape(-1)


def solution(mesh):
    return jax.shard_map(
        on_device,
        mesh=mesh,
        in_specs=(P(("dp", "sub"), None), P(), P()),
        out_specs=(P(("dp", "sub"), None), P(("dp", "sub")), P(("dp", "sub"))),
        check_vma=False,
    )
```
